512 devices in a mesh: row: 16 (over z, core), col: 8 (over y), layer: 4 (over x).
Axes of the slice: x: 4, y: 8, z: 8, core: 2. Of those that a mesh axis runs over, the one named last changes fastest.
Arguments:
- left_slab: float32 [4, 8192, 2048], P('layer', 'row', 'col'), may hold values from -6 to 6
- right_window: float32 [4, 2048, 8192], P('layer', 'row', 'col'), may hold values from -0.0625 to 0.0625
- left_pattern: int32 [4, 128, 32], P('layer', 'row', 'col'), may hold values 0 or 1
- right_pattern: int32 [4, 32, 128], P('layer', 'row', 'col'), may hold values from 0 to 1, as said below
- square_blocks: float32 [8192, 8192], P(('row', 'layer'), 'col'), may hold values from -6 to 6
- result_pattern: int32 [128, 128], P('row', 'col'), may hold values 0 or 1
Outputs:
- purified: float32 [8192, 8192], P(('row', 'layer'), 'col')
The draws below stay inside these ranges and needn't reach their ends.
Inputs may be any that keep to these rules, and one draw needn't show every extreme that they name: `right_pattern`: for each group and each tile of 32 // 16 inner blocks by 16 block columns (the tiles aligned with those sizes), exactly three quarters of the tile's blocks are 1.
All inputs are finite; a program needn't handle non-finite values. No bound on the sum of `left_pattern` or of `result_pattern` on one device may be relied on, other than what follows from the above.
Results may differ from the reference program's by a relative error of at most 0.0001.
Values sent between devices are 32-bit elements; how exact they have to be, the bound alone decides.
No kernel may reach another device: no remote copies, remote signals or barrier semaphores. Data moves between devices by JAX's collectives and lax.ppermute only.
A program may use at most 128 MiB of HBM per device.

```python
import jax
import jax.numpy as jnp
from jax import lax

BS = 64
CB_DEV = 16
RBLOCKS = 128
IBLOCKS = 32
CBLOCKS = 128
ROWS = 8192
INNER = 2048
COLUMNS = 8192
N_ROW = 16
N_COL = 8
N_LAYER = 4


def draw_right_pattern(key, part):
    key = jax.random.fold_in(key, 7)
    height = IBLOCKS // N_ROW
    tile = height * CB_DEV
    count = N_LAYER * N_ROW * N_COL
    noise = jax.random.randint(key, (count, tile), 0, 1 << 20)
    scores = noise * tile + jnp.arange(tile, dtype=jnp.int32)[None, :]
    ranks = jnp.argsort(jnp.argsort(scores, axis=1), axis=1)
    flags = (ranks < 3 * tile // 4).astype(jnp.int32)
    flags = flags.reshape(N_LAYER, N_ROW, N_COL, height, CB_DEV).transpose(0, 1, 3, 2, 4)
    return flags.reshape(N_LAYER, IBLOCKS, CBLOCKS)


def with_ends(entries, rng, low, high):
    extent = entries.shape
    index_at = [jax.random.randint(jax.random.fold_in(rng, axis), (), 0, extent[axis]) for axis in range(len(extent))]
    entries = entries.at[tuple(index_at)].set(low)
    longest = extent.index(max(extent))
    index_at[longest] = (index_at[longest] + 1) % extent[longest]
    return entries.at[tuple(index_at)].set(high)


def steps_of(stream_key, extent, pieces, low, largest):
    factor_of = 1.0
    for axis_at, parts in pieces:
        draws = jax.random.uniform(jax.random.fold_in(jax.random.fold_in(stream_key, 6), axis_at), (parts,), jnp.float32, low / len(pieces), largest / len(pieces))
        factor_of = factor_of * jnp.repeat(jnp.exp(draws), extent[axis_at] // parts).reshape((-1,) + (1,) * (len(extent) - 1 - axis_at))
    return factor_of


def normal_values(stream_key, dims, spread, most, cuts=(), kind=jnp.bfloat16):
    drawn = spread * jax.random.normal(stream_key, dims, jnp.float32)
    if cuts:
        drawn = drawn * steps_of(stream_key, dims, cuts, -0.22, 0.18)
    return jnp.clip(drawn, -most, most).astype(kind)


def setup_inputs(seed: int = 0) -> dict:
    streams_of = jax.random.split(jax.random.key(seed), 7)
    left_slab = normal_values(streams_of[0], (N_LAYER, ROWS, INNER), 1.0, 6.0, ((0, 4), (1, 16), (2, 8)), jnp.float32)
    right_window = normal_values(streams_of[1], (N_LAYER, INNER, COLUMNS), (N_LAYER * INNER) ** -0.5, 0.0625, ((0, 4), (1, 16), (2, 8)), jnp.float32)
    left_pattern = with_ends((jax.random.randint(streams_of[2], (N_LAYER, RBLOCKS, IBLOCKS), 0, 4) < 3).astype(jnp.int32), jax.random.fold_in(streams_of[2], 1), 0, 1)
    right_pattern = draw_right_pattern(jax.random.fold_in(streams_of[6], 71), 0)
    square_blocks = normal_values(streams_of[4], (ROWS, COLUMNS), 1.0, 6.0, ((0, 64), (1, 8)), jnp.float32)
    result_pattern = with_ends((jax.random.randint(streams_of[5], (RBLOCKS, CBLOCKS), 0, 4) < 3).astype(jnp.int32), jax.random.fold_in(streams_of[5], 1), 0, 1)
    return dict(left_slab=left_slab, right_window=right_window, left_pattern=left_pattern, right_pattern=right_pattern, square_blocks=square_blocks, result_pattern=result_pattern)


def widen(pattern, size):
    lead = pattern.shape[:-2]
    height, breadth = pattern.shape[-2], pattern.shape[-1]
    flags = pattern.astype(jnp.float32)[..., :, None, :, None]
    flags = jnp.broadcast_to(flags, lead + (height, size, breadth, size))
    return flags.reshape(lead + (height * size, breadth * size))


def reference(left_slab, right_window, left_pattern, right_pattern, square_blocks, result_pattern):
    masked_left = left_slab * widen(left_pattern, BS)
    masked_right = right_window * widen(right_pattern, BS)
    cube = jnp.zeros((masked_left.shape[1], masked_right.shape[2]), jnp.float32)
    for group in range(N_LAYER):
        cube = cube + jnp.dot(masked_left[group], masked_right[group], precision=lax.Precision.HIGHEST, preferred_element_type=jnp.float32)
    return widen(result_pattern, BS) * (3.0 * square_blocks - 2.0 * cube)
```

```python
import jax
import jax.numpy as jnp
from jax import lax
from jax.experimental import pallas as pl
from jax.experimental.pallas import tpu as pltpu
from jax.sharding import PartitionSpec as P

BS = 64
LANES = 128
MAIN = 24
EXTRA = 8
ROWS_MAIN = 6 * LANES
PACKED = ROWS_MAIN + 16
BF = jnp.bfloat16
F32 = jnp.float32


def lane_half():
    return lax.broadcasted_iota(jnp.int32, (BS, LANES), 1) // BS


def pair_mask(low, high):
    return jnp.where(lane_half() == 0, low.astype(F32), high.astype(F32))


def mask_left_kernel(flags, x, out):
    for i in range(8):
        for c in range(2):
            mask = pair_mask(flags[i, 2 * c], flags[i, 2 * c + 1])
            at = (pl.ds(i * BS, BS), pl.ds(c * LANES, LANES))
            out[at] = x[at] * mask


def mask_left(x, flags):
    return pl.pallas_call(
        mask_left_kernel,
        out_shape=jax.ShapeDtypeStruct(x.shape, F32),
        in_specs=[pl.BlockSpec(memory_space=pltpu.SMEM), pl.BlockSpec(memory_space=pltpu.VMEM)],
        out_specs=pl.BlockSpec(memory_space=pltpu.VMEM),
    )(flags, x)


def pack_kernel(flags, x, out, holes, homes):
    for c in range(6):
        out[pl.ds(c * LANES, LANES), :] = x[:, pl.ds(c * LANES, LANES)]
    count = jnp.int32(0)
    for s in range(MAIN):
        holes[count] = s
        count = count + jnp.where(flags[s // 12, s % 12] == 0, 1, 0)
    used = jnp.int32(0)
    half = lane_half()
    for e in range(EXTRA):
        kept = flags[e // 4, 12 + e % 4] != 0
        slot = holes[jnp.minimum(used, EXTRA)]
        homes[e] = jnp.where(kept, slot, MAIN)
        used = used + jnp.where(kept, 1, 0)

        @pl.when(kept)
        def _():
            column = slot % 12
            at = pl.ds(pl.multiple_of((column // 2) * LANES + (slot // 12) * BS, BS), BS)
            block = x[pl.ds((e // 4) * BS, BS), pl.ds((6 + (e % 4) // 2) * LANES, LANES)]
            turned = pltpu.roll(block, BS, 1)
            side = column % 2
            block = jnp.where(side == e % 2, block, turned)
            out[at, :] = jnp.where(half == side, block, out[at, :])

    lane = lax.broadcasted_iota(jnp.int32, (1, LANES), 1)
    row = jnp.zeros((1, LANES), F32)
    for e in range(EXTRA):
        row = jnp.where(lane == e, homes[e].astype(F32), row)
    out[pl.ds(ROWS_MAIN, 1), :] = row
    for b in range(2):
        for c in range(6):
            mask = jnp.where(lane < BS, flags[b, 2 * c].astype(F32), flags[b, 2 * c + 1].astype(F32))
            out[pl.ds(ROWS_MAIN + 1 + b * 6 + c, 1), :] = mask
    out[pl.ds(ROWS_MAIN + 13, 3), :] = jnp.zeros((3, LANES), F32)


def pack_right(x, flags):
    return pl.pallas_call(
        pack_kernel,
        out_shape=jax.ShapeDtypeStruct((PACKED, LANES), F32),
        in_specs=[pl.BlockSpec(memory_space=pltpu.SMEM), pl.BlockSpec(memory_space=pltpu.VMEM)],
        out_specs=pl.BlockSpec(memory_space=pltpu.VMEM),
        scratch_shapes=[pltpu.SMEM((MAIN + 1,), jnp.int32), pltpu.SMEM((EXTRA,), jnp.int32)],
    )(flags, x)


def split(x):
    high = x.astype(BF)
    return high, (x - high.astype(F32)).astype(BF)


def unpack_kernel(homes, x, high, low):
    z = pl.program_id(0)
    half = lane_half()

    def store(b, c, value):
        at = (pl.ds(b * BS, BS), pl.ds(c * LANES, LANES))
        high[at], low[at] = split(value)

    for b in range(2):
        for c in range(6):
            mask = x[0, pl.ds(ROWS_MAIN + 1 + b * 6 + c, 1), :]
            store(b, c, x[0, pl.ds(c * LANES + b * BS, BS), :] * mask)
        for c in range(2):
            sides = []
            for k in range(2):
                slot = homes[z, b * 4 + 2 * c + k]
                kept = slot < MAIN
                slot = jnp.minimum(slot, MAIN - 1)
                column = slot % 12
                at = pl.ds(pl.multiple_of((column // 2) * LANES + (slot // 12) * BS, BS), BS)
                block = x[0, at, :]
                block = jnp.where(column % 2 == k, block, pltpu.roll(block, BS, 1))
                sides.append(jnp.where(kept, block, 0.0))
            store(b, 6 + c, jnp.where(half == 0, sides[0], sides[1]))


def unpack_right(packed, homes):
    shape = jax.ShapeDtypeStruct((16 * LANES, 1024), BF)
    block = pl.BlockSpec((LANES, 1024), lambda z, *_: (z, 0))
    return pl.pallas_call(
        unpack_kernel,
        out_shape=(shape, shape),
        grid_spec=pltpu.PrefetchScalarGridSpec(
            num_scalar_prefetch=1,
            grid=(16,),
            in_specs=[pl.BlockSpec((1, PACKED, LANES), lambda z, *_: (z, 0, 0))],
            out_specs=(block, block),
        ),
    )(homes, packed)


def product_kernel(where, *refs):
    parts, (right_high, right_low, out, left_high, left_low) = refs[:9], refs[9:]

    @pl.when(pl.program_id(0) == 0)
    def _():
        for n, part in enumerate(parts):
            first = 256 if n == 8 else 0
            at = (pl.ds(first, part.shape[0]), pl.ds(pl.multiple_of(where[min(n, 7)] * 256, 256), 256))
            left_high[at], left_low[at] = split(part[...])

    total = jnp.dot(left_low[...], right_high[...], preferred_element_type=F32)
    total += jnp.dot(left_high[...], right_low[...], preferred_element_type=F32)
    total += jnp.dot(left_high[...], right_high[...], preferred_element_type=F32)
    out[...] = total


def product(parts, where, right_high, right_low):
    width = 256
    right = pl.BlockSpec((2048, width), lambda j, *_: (0, j))
    return pl.pallas_call(
        product_kernel,
        out_shape=jax.ShapeDtypeStruct((512, 1024), F32),
        grid_spec=pltpu.PrefetchScalarGridSpec(
            num_scalar_prefetch=1,
            grid=(1024 // width,),
            in_specs=[pl.BlockSpec(p.shape, lambda j, *_: (0, 0)) for p in parts] + [right, right],
            out_specs=pl.BlockSpec((512, width), lambda j, *_: (0, j)),
            scratch_shapes=[pltpu.VMEM((512, 2048), BF)] * 2,
        ),
        compiler_params=pltpu.CompilerParams(vmem_limit_bytes=40 << 20),
    )(where, *parts, right_high, right_low)


def finish_kernel(where, flags, terms, square, out):
    for b in range(2):
        for c in range(8):
            at = (pl.ds(b * BS, BS), pl.ds(c * LANES, LANES))
            total = (terms[(0,) + at] + terms[(1,) + at]) + (terms[(2,) + at] + terms[(3,) + at])
            line = where[0] * 2 + b
            mask = pair_mask(flags[line, 2 * c], flags[line, 2 * c + 1])
            out[at] = mask * (3.0 * square[at] - 2.0 * total)


def finish(terms, square, flags, where):
    smem = pl.BlockSpec(memory_space=pltpu.SMEM)
    vmem = pl.BlockSpec(memory_space=pltpu.VMEM)
    return pl.pallas_call(
        finish_kernel,
        out_shape=jax.ShapeDtypeStruct(square.shape, F32),
        in_specs=[smem, smem, vmem, vmem],
        out_specs=vmem,
    )(where, flags, terms, square)


def shift(n, by):
    return [(i, (i + by) % n) for i in range(n)]


def gather_left(own):
    def send(x, by):
        return lax.ppermute(x, "col", shift(8, by))

    up1, down1 = send(own, 1), send(own, -1)
    up2, down2 = send(own, 2), send(own, -2)
    up3, down3 = send(up2, 1), send(down2, -1)
    far_a, far_b = send(up2[:256], 2), send(down2[256:], -2)
    return [own, up1, down1, up2, down2, up3, down3, far_a, far_b]


def local(left_slab, right_window, left_pattern, right_pattern, square_blocks, result_pattern):
    packed = pack_right(right_window[0], right_pattern[0])
    packed = lax.all_gather(packed, "row", axis=0, tiled=False)
    parts = gather_left(mask_left(left_slab[0], left_pattern[0]))
    homes = packed[:, ROWS_MAIN, :EXTRA].astype(jnp.int32)
    right_high, right_low = unpack_right(packed, homes)
    me = lax.axis_index("col")
    where = jnp.stack([lax.rem(me + d, 8) for d in (8, 7, 9, 6, 10, 5, 11, 12)])
    cube = product(parts, where, right_high, right_low)
    terms = lax.all_to_all(cube.reshape(4, 128, 1024), "layer", 0, 0)
    layer = lax.axis_index("layer").reshape((1,))
    return finish(terms, square_blocks, result_pattern, layer)


def solution(mesh):
    in_specs = (
        P("layer", "row", "col"),
        P("layer", "row", "col"),
        P("layer", "row", "col"),
        P("layer", "row", "col"),
        P(("row", "layer"), "col"),
        P("row", "col"),
    )
    out_specs = P(("row", "layer"), "col")
    return jax.shard_map(local, mesh=mesh, in_specs=in_specs, out_specs=out_specs, check_vma=False)
```

```python
import functools

import jax
import jax.numpy as jnp
from jax import lax
from jax.experimental import pallas as pl
from jax.experimental.pallas import tpu as pltpu
from jax.sharding import PartitionSpec as P

BS = 64
LANES = 128
MAIN = 24
EXTRA = 8
META = 16
PACKED = META + 6 * LANES
BF = jnp.bfloat16
F32 = jnp.float32


def lane_half():
    return lax.broadcasted_iota(jnp.int32, (BS, LANES), 1) // BS


def pair_mask(low, high):
    return jnp.where(lane_half() == 0, low.astype(F32), high.astype(F32))


def mask_left_kernel(flags, x, out):
    for i in range(8):
        for c in range(2):
            mask = pair_mask(flags[2 * c, i], flags[2 * c + 1, i])
            at = (pl.ds(i * BS, BS), pl.ds(c * LANES, LANES))
            out[at] = x[at] * mask


def mask_left(x, flags):
    return pl.pallas_call(
        mask_left_kernel,
        out_shape=jax.ShapeDtypeStruct(x.shape, F32),
        in_specs=[pl.BlockSpec(memory_space=pltpu.SMEM), pl.BlockSpec(memory_space=pltpu.VMEM)],
        out_specs=pl.BlockSpec(memory_space=pltpu.VMEM),
    )(flags, x)


def pack_kernel(flags, x, out, holes):
    for c in range(6):
        out[pl.ds(META + c * LANES, LANES), :] = x[:, pl.ds(c * LANES, LANES)]
    count = jnp.int32(0)
    for s in range(MAIN):
        holes[count] = s
        count = count + jnp.where(flags[(s >> 1) & 1, 2 * (s >> 2) + (s & 1)] == 0, 1, 0)
    used = jnp.int32(0)
    half = lane_half()
    lane = lax.broadcasted_iota(jnp.int32, (1, LANES), 1)
    row = jnp.zeros((1, LANES), F32)
    for e in range(EXTRA):
        kept = flags[e >> 2, 12 + (e & 3)] != 0
        slot = holes[jnp.minimum(used, EXTRA)]
        row = jnp.where(lane == e, jnp.where(kept, slot, -1).astype(F32), row)
        used = used + jnp.where(kept, 1, 0)

        @pl.when(kept)
        def _():
            at = pl.ds(pl.multiple_of(META + (slot >> 1) * BS, 16), BS)
            block = x[pl.ds((e >> 2) * BS, BS), pl.ds((6 + ((e >> 1) & 1)) * LANES, LANES)]
            side = slot & 1
            block = jnp.where(side == (e & 1), block, pltpu.roll(block, BS, 1))
            out[at, :] = jnp.where(half == side, block, out[at, :])

    out[pl.ds(0, 1), :] = row
    for c in range(6):
        for b in range(2):
            mask = jnp.where(lane < BS, flags[b, 2 * c].astype(F32), flags[b, 2 * c + 1].astype(F32))
            out[pl.ds(1 + c * 2 + b, 1), :] = mask
    out[pl.ds(13, 3), :] = jnp.zeros((3, LANES), F32)


def pack_right(x, flags):
    return pl.pallas_call(
        pack_kernel,
        out_shape=jax.ShapeDtypeStruct((PACKED, LANES), F32),
        in_specs=[pl.BlockSpec(memory_space=pltpu.SMEM), pl.BlockSpec(memory_space=pltpu.VMEM)],
        out_specs=pl.BlockSpec(memory_space=pltpu.VMEM),
        scratch_shapes=[pltpu.SMEM((MAIN + 1,), jnp.int32)],
    )(flags, x)


def split(x):
    high = x.astype(BF)
    return high, (x - high.astype(F32)).astype(BF)


def product_kernel(side, where, packed, *refs):
    parts, (out, tiles, lefts, high0, high1, low0, low1, homes, tile_sems, left_sems, home_sem) = refs[:9], refs[9:]
    need = tiles.shape[2]
    copies = []
    if side:
        home_copy = pltpu.make_async_copy(packed.at[:, pl.ds(0, 8), :], homes, home_sem)
        home_copy.start()
    for k in range(8):
        tile = pltpu.make_async_copy(packed.at[pl.ds(where[k] * 2, 2), pl.ds(0, need), :], tiles.at[k], tile_sems.at[k])
        tile.start()
        if k < 7:
            pieces = [pltpu.make_async_copy(parts[k], lefts.at[k], left_sems.at[k])]
        else:
            pieces = [
                pltpu.make_async_copy(parts[7 + h], lefts.at[7, pl.ds(h * 256, 256)], left_sems.at[7 + h]) for h in range(2)
            ]
        for piece in pieces:
            piece.start()
        copies.append([tile] + pieces)
    half = lane_half()
    if side:
        home_copy.wait()

    def unpack(k):
        high, low = (high0, low0) if k % 2 == 0 else (high1, low1)
        for z in range(2):
            for b in range(2):
                for c in range(4):
                    pair = 4 * side + c
                    if pair < 6:
                        mask = tiles[k, z, pl.ds(1 + pair * 2 + b, 1), :]
                        value = tiles[k, z, pl.ds(META + pair * LANES + b * BS, BS), :] * mask
                    else:
                        halves = []
                        for h in range(2):
                            slot = homes[where[k] * 2 + z, 0, b * 4 + 2 * (pair - 6) + h].astype(jnp.int32)
                            kept = slot >= 0
                            slot = jnp.maximum(slot, 0)
                            block = tiles[k, z, pl.ds(pl.multiple_of(META + (slot >> 1) * BS, 16), BS), :]
                            block = jnp.where((slot & 1) == h, block, pltpu.roll(block, BS, 1))
                            halves.append(jnp.where(kept, block, 0.0))
                        value = jnp.where(half == 0, halves[0], halves[1])
                    at = (pl.ds(z * LANES + b * BS, BS), pl.ds(c * LANES, LANES))
                    high[at], low[at] = split(value)
        return high, low

    for k in range(8):
        for copy in copies[k]:
            copy.wait()
        high, low = unpack(k)
        left_high, left_low = split(lefts[k])
        total = jnp.dot(left_low, high[...], preferred_element_type=F32)
        total += jnp.dot(left_high, low[...], preferred_element_type=F32)
        total += jnp.dot(left_high, high[...], preferred_element_type=F32)
        if k:
            total += out[...]
        out[...] = total


def product(side, parts, where, packed):
    smem = pl.BlockSpec(memory_space=pltpu.SMEM)
    hbm = pl.BlockSpec(memory_space=pltpu.HBM)
    need = PACKED if side else META + 4 * LANES
    return pl.pallas_call(
        functools.partial(product_kernel, side),
        out_shape=jax.ShapeDtypeStruct((512, 512), F32),
        in_specs=[smem] + [hbm] * 10,
        out_specs=pl.BlockSpec(memory_space=pltpu.VMEM),
        scratch_shapes=[
            pltpu.VMEM((8, 2, need, LANES), F32),
            pltpu.VMEM((8, 512, 256), F32),
            pltpu.VMEM((256, 512), BF),
            pltpu.VMEM((256, 512), BF),
            pltpu.VMEM((256, 512), BF),
            pltpu.VMEM((256, 512), BF),
            pltpu.SMEM((16, 8, LANES), F32),
            pltpu.SemaphoreType.DMA((8,)),
            pltpu.SemaphoreType.DMA((9,)),
            pltpu.SemaphoreType.DMA,
        ],
        cost_estimate=pl.CostEstimate(flops=6 * 512 * 512 * 2048, bytes_accessed=9 << 20, transcendentals=0),
        compiler_params=pltpu.CompilerParams(vmem_limit_bytes=56 << 20),
    )(where, packed, *parts)


def finish_kernel(side, where, flags, terms, square, *refs):
    out = refs[-1]
    for b in range(2):
        for c in range(4):
            at = (pl.ds(b * BS, BS), pl.ds(c * LANES, LANES))
            total = (terms[(0,) + at] + terms[(1,) + at]) + (terms[(2,) + at] + terms[(3,) + at])
            line, column = where[0] * 2 + b, 8 * side + 2 * c
            mask = pair_mask(flags[line, column], flags[line, column + 1])
            out[at] = mask * (3.0 * square[at] - 2.0 * total)


def finish(side, terms, square, flags, where, *before):
    smem = pl.BlockSpec(memory_space=pltpu.SMEM)
    half = pl.BlockSpec((128, 512), lambda i: (0, side))
    return pl.pallas_call(
        functools.partial(finish_kernel, side),
        out_shape=jax.ShapeDtypeStruct(square.shape, F32),
        grid=(1,),
        in_specs=[smem, smem, pl.BlockSpec((4, 128, 512), lambda i: (0, 0, 0)), half]
        + [pl.BlockSpec(memory_space=pltpu.HBM)] * len(before),
        out_specs=half,
        input_output_aliases={4: 0} if before else {},
        cost_estimate=pl.CostEstimate(flops=1 << 20, bytes_accessed=2 << 20, transcendentals=0),
    )(where, flags, terms, square, *before)


def shift(n, by):
    return [(i, (i + by) % n) for i in range(n)]


def gather_left(own):
    def send(x, by):
        return lax.ppermute(x, "col", shift(8, by))

    up1, down1 = send(own, 1), send(own, -1)
    up2, down2 = send(own, 2), send(own, -2)
    up3, down3 = send(up2, 1), send(down2, -1)
    far_a, far_b = send(up2[:256], 2), send(down2[256:], -2)
    return [own, up1, down1, up2, down2, up3, down3, far_a, far_b]


def local(left_slab, right_window, left_pattern, right_pattern, square_blocks, result_pattern):
    packed = pack_right(right_window[0], right_pattern[0])
    packed = lax.all_gather(packed, "row", axis=0, tiled=False)
    parts = gather_left(mask_left(left_slab[0], left_pattern[0].T))
    me = lax.axis_index("col")
    where = lax.rem(me + jnp.array([8, 7, 9, 6, 10, 5, 11, 12], jnp.int32), 8)
    layer = lax.axis_index("layer").reshape((1,))
    out = ()
    for side in range(2):
        cube = product(side, parts, where, packed)
        terms = lax.all_to_all(cube.reshape(4, 128, 512), "layer", 0, 0)
        out = (finish(side, terms, square_blocks, result_pattern, layer, *out),)
    return out[0]


def solution(mesh):
    in_specs = (
        P("layer", "row", "col"),
        P("layer", "row", "col"),
        P("layer", "row", "col"),
        P("layer", "row", "col"),
        P(("row", "layer"), "col"),
        P("row", "col"),
    )
    out_specs = P(("row", "layer"), "col")
    return jax.shard_map(local, mesh=mesh, in_specs=in_specs, out_specs=out_specs, check_vma=False)
```

```python
import functools

import jax
import jax.numpy as jnp
from jax import lax
from jax.experimental import pallas as pl
from jax.experimental.pallas import tpu as pltpu
from jax.sharding import PartitionSpec as P

BS = 64
LANES = 128
MAIN = 24
EXTRA = 8
META = 16
PACKED = META + 6 * LANES
BF = jnp.bfloat16
F32 = jnp.float32


def lane_half():
    return lax.broadcasted_iota(jnp.int32, (BS, LANES), 1) // BS


def pair_mask(low, high):
    return jnp.where(lane_half() == 0, low.astype(F32), high.astype(F32))


def prepare_kernel(left_flags, left, flags, x, left_out, out, holes):
    for i in range(8):
        for c in range(2):
            mask = pair_mask(left_flags[2 * c, i], left_flags[2 * c + 1, i])
            at = (pl.ds(i * BS, BS), pl.ds(c * LANES, LANES))
            left_out[at] = left[at] * mask
    for c in range(6):
        out[pl.ds(META + c * LANES, LANES), :] = x[:, pl.ds(c * LANES, LANES)]
    count = jnp.int32(0)
    for s in range(MAIN):
        holes[count] = s
        count = count + jnp.where(flags[(s >> 1) & 1, 2 * (s >> 2) + (s & 1)] == 0, 1, 0)
    used = jnp.int32(0)
    half = lane_half()
    lane = lax.broadcasted_iota(jnp.int32, (1, LANES), 1)
    row = jnp.zeros((1, LANES), F32)
    for e in range(EXTRA):
        kept = flags[e >> 2, 12 + (e & 3)] != 0
        slot = holes[jnp.minimum(used, EXTRA)]
        row = jnp.where(lane == e, jnp.where(kept, slot, -1).astype(F32), row)
        used = used + jnp.where(kept, 1, 0)

        @pl.when(kept)
        def _():
            at = pl.ds(pl.multiple_of(META + (slot >> 1) * BS, 16), BS)
            block = x[pl.ds((e >> 2) * BS, BS), pl.ds((6 + ((e >> 1) & 1)) * LANES, LANES)]
            side = slot & 1
            block = jnp.where(side == (e & 1), block, pltpu.roll(block, BS, 1))
            out[at, :] = jnp.where(half == side, block, out[at, :])

    out[pl.ds(0, 1), :] = row
    for c in range(6):
        for b in range(2):
            mask = jnp.where(lane < BS, flags[b, 2 * c].astype(F32), flags[b, 2 * c + 1].astype(F32))
            out[pl.ds(1 + c * 2 + b, 1), :] = mask
    out[pl.ds(13, 3), :] = jnp.zeros((3, LANES), F32)


def prepare(left, left_flags, right, right_flags):
    smem = pl.BlockSpec(memory_space=pltpu.SMEM)
    vmem = pl.BlockSpec(memory_space=pltpu.VMEM)
    return pl.pallas_call(
        prepare_kernel,
        out_shape=(jax.ShapeDtypeStruct(left.shape, F32), jax.ShapeDtypeStruct((PACKED, LANES), F32)),
        in_specs=[smem, vmem, smem, vmem],
        out_specs=(vmem, vmem),
        scratch_shapes=[pltpu.SMEM((MAIN + 1,), jnp.int32)],
    )(left_flags, left, right_flags, right)


def split(x):
    high = x.astype(BF)
    return high, (x - high.astype(F32)).astype(BF)


def product_kernel(side, first, last, where, packed, *refs):
    steps = range(first, last)
    count = sum(2 if k == 7 else 1 for k in steps)
    parts, refs = refs[:count], refs[count:]
    if first:
        before, refs = refs[0], refs[1:]
    out, tiles, lefts, high0, high1, low0, low1, homes, tile_sems, left_sems, home_sem = refs
    need = tiles.shape[2]
    copies = {}
    if side:
        home_copy = pltpu.make_async_copy(packed.at[:, pl.ds(0, 8), :], homes, home_sem)
        home_copy.start()
    for k in steps:
        n = k - first
        tile = pltpu.make_async_copy(packed.at[pl.ds(where[k] * 2, 2), pl.ds(0, need), :], tiles.at[n], tile_sems.at[n])
        tile.start()
        if k < 7:
            pieces = [pltpu.make_async_copy(parts[n], lefts.at[n], left_sems.at[n])]
        else:
            pieces = [
                pltpu.make_async_copy(parts[n + h], lefts.at[n, pl.ds(h * 256, 256)], left_sems.at[n + h]) for h in range(2)
            ]
        for piece in pieces:
            piece.start()
        copies[k] = [tile] + pieces
    half = lane_half()
    if side:
        home_copy.wait()

    def unpack(k):
        n = k - first
        high, low = (high0, low0) if n % 2 == 0 else (high1, low1)
        for z in range(2):
            for b in range(2):
                for c in range(4):
                    pair = 4 * side + c
                    if pair < 6:
                        mask = tiles[n, z, pl.ds(1 + pair * 2 + b, 1), :]
                        value = tiles[n, z, pl.ds(META + pair * LANES + b * BS, BS), :] * mask
                    else:
                        halves = []
                        for h in range(2):
                            slot = homes[where[k] * 2 + z, 0, b * 4 + 2 * (pair - 6) + h].astype(jnp.int32)
                            kept = slot >= 0
                            slot = jnp.maximum(slot, 0)
                            block = tiles[n, z, pl.ds(pl.multiple_of(META + (slot >> 1) * BS, 16), BS), :]
                            block = jnp.where((slot & 1) == h, block, pltpu.roll(block, BS, 1))
                            halves.append(jnp.where(kept, block, 0.0))
                        value = jnp.where(half == 0, halves[0], halves[1])
                    at = (pl.ds(z * LANES + b * BS, BS), pl.ds(c * LANES, LANES))
                    high[at], low[at] = split(value)
        return high, low

    for k in steps:
        for copy in copies[k]:
            copy.wait()
        high, low = unpack(k)
        left_high, left_low = split(lefts[k - first])
        total = jnp.dot(left_low, high[...], preferred_element_type=F32)
        total += jnp.dot(left_high, low[...], preferred_element_type=F32)
        total += jnp.dot(left_high, high[...], preferred_element_type=F32)
        if k > first:
            total += out[...]
        elif first:
            total += before[...]
        out[...] = total


def product(side, first, last, parts, where, packed, *before):
    smem = pl.BlockSpec(memory_space=pltpu.SMEM)
    hbm = pl.BlockSpec(memory_space=pltpu.HBM)
    vmem = pl.BlockSpec(memory_space=pltpu.VMEM)
    need = PACKED if side else META + 4 * LANES
    steps = last - first
    half = pltpu.VMEM((256, 512), BF)
    return pl.pallas_call(
        functools.partial(product_kernel, side, first, last),
        out_shape=jax.ShapeDtypeStruct((512, 512), F32),
        in_specs=[smem] + [hbm] * (1 + len(parts)) + [vmem] * len(before),
        out_specs=vmem,
        scratch_shapes=[
            pltpu.VMEM((steps, 2, need, LANES), F32),
            pltpu.VMEM((steps, 512, 256), F32),
            half,
            half,
            half,
            half,
            pltpu.SMEM((16, 8, LANES), F32),
            pltpu.SemaphoreType.DMA((steps,)),
            pltpu.SemaphoreType.DMA((steps + 1,)),
            pltpu.SemaphoreType.DMA,
        ],
        cost_estimate=pl.CostEstimate(flops=6 * 512 * 512 * 256 * steps, bytes_accessed=steps << 20, transcendentals=0),
        compiler_params=pltpu.CompilerParams(vmem_limit_bytes=56 << 20),
    )(where, packed, *parts, *before)


def finish_kernel(side, where, flags, terms, square, *refs):
    out = refs[-1]
    for b in range(2):
        for c in range(4):
            at = (pl.ds(b * BS, BS), pl.ds(c * LANES, LANES))
            total = (terms[(0,) + at] + terms[(1,) + at]) + (terms[(2,) + at] + terms[(3,) + at])
            line, column = where[0] * 2 + b, 8 * side + 2 * c
            mask = pair_mask(flags[line, column], flags[line, column + 1])
            out[at] = mask * (3.0 * square[at] - 2.0 * total)


def finish(side, terms, square, flags, where, *before):
    smem = pl.BlockSpec(memory_space=pltpu.SMEM)
    half = pl.BlockSpec((128, 512), lambda i: (0, side))
    return pl.pallas_call(
        functools.partial(finish_kernel, side),
        out_shape=jax.ShapeDtypeStruct(square.shape, F32),
        grid=(1,),
        in_specs=[smem, smem, pl.BlockSpec((4, 128, 512), lambda i: (0, 0, 0)), half]
        + [pl.BlockSpec(memory_space=pltpu.HBM)] * len(before),
        out_specs=half,
        input_output_aliases={4: 0} if before else {},
        cost_estimate=pl.CostEstimate(flops=1 << 20, bytes_accessed=2 << 20, transcendentals=0),
    )(where, flags, terms, square, *before)


def shift(n, by):
    return [(i, (i + by) % n) for i in range(n)]


def gather_left(own):
    def send(x, by):
        return lax.ppermute(x, "col", shift(8, by))

    up1, down1 = send(own, 1), send(own, -1)
    up2, down2 = send(up1, 1), send(down1, -1)
    up3, down3 = send(up2, 1), send(down2, -1)
    far_a, far_b = send(up3[:256], 1), send(down3[256:], -1)
    return [own, up1, down1, up2, down2, up3, down3, far_a, far_b]


def local(left_slab, right_window, left_pattern, right_pattern, square_blocks, result_pattern):
    left, packed = prepare(left_slab[0], left_pattern[0].T, right_window[0], right_pattern[0])
    packed = lax.all_gather(packed, "row", axis=0, tiled=False)
    parts = gather_left(left)
    me = lax.axis_index("col")
    where = lax.rem(me + jnp.array([8, 7, 9, 6, 10, 5, 11, 12], jnp.int32), 8)
    layer = lax.axis_index("layer").reshape((1,))
    out = ()
    for side in range(2):
        if side:
            cube = product(side, 0, 8, parts, where, packed)
        else:
            cube = product(side, 0, 7, parts[:7], where, packed)
            cube = product(side, 7, 8, parts[7:], where, packed, cube)
        terms = lax.all_to_all(cube.reshape(4, 128, 512), "layer", 0, 0)
        out = (finish(side, terms, square_blocks, result_pattern, layer, *out),)
    return out[0]


def solution(mesh):
    in_specs = (
        P("layer", "row", "col"),
        P("layer", "row", "col"),
        P("layer", "row", "col"),
        P("layer", "row", "col"),
        P(("row", "layer"), "col"),
        P("row", "col"),
    )
    out_specs = P(("row", "layer"), "col")
    return jax.shard_map(local, mesh=mesh, in_specs=in_specs, out_specs=out_specs, check_vma=False)
```

```python
import functools

import jax
import jax.numpy as jnp
from jax import lax
from jax.experimental import pallas as pl
from jax.experimental.pallas import tpu as pltpu
from jax.sharding import PartitionSpec as P

BS = 64
LANES = 128
MAIN = 24
EXTRA = 8
META = 16
PACKED = META + 6 * LANES
BF = jnp.bfloat16
F32 = jnp.float32


def lane_half():
    return lax.broadcasted_iota(jnp.int32, (BS, LANES), 1) // BS


def pair_mask(low, high):
    return jnp.where(lane_half() == 0, low.astype(F32), high.astype(F32))


def prepare_kernel(left_flags, left, flags, x, left_out, out, holes):
    for i in range(8):
        for c in range(2):
            mask = pair_mask(left_flags[2 * c, i], left_flags[2 * c + 1, i])
            at = (pl.ds(i * BS, BS), pl.ds(c * LANES, LANES))
            left_out[at] = left[at] * mask
    for c in range(6):
        out[pl.ds(META + c * LANES, LANES), :] = x[:, pl.ds(c * LANES, LANES)]
    count = jnp.int32(0)
    for s in range(MAIN):
        holes[count] = s
        count = count + jnp.where(flags[(s >> 1) & 1, 2 * (s >> 2) + (s & 1)] == 0, 1, 0)
    used = jnp.int32(0)
    half = lane_half()
    lane = lax.broadcasted_iota(jnp.int32, (1, LANES), 1)
    row = jnp.zeros((1, LANES), F32)
    for e in range(EXTRA):
        kept = flags[e >> 2, 12 + (e & 3)] != 0
        slot = holes[jnp.minimum(used, EXTRA)]
        row = jnp.where(lane == e, jnp.where(kept, slot, -1).astype(F32), row)
        used = used + jnp.where(kept, 1, 0)

        @pl.when(kept)
        def _():
            at = pl.ds(pl.multiple_of(META + (slot >> 1) * BS, 16), BS)
            block = x[pl.ds((e >> 2) * BS, BS), pl.ds((6 + ((e >> 1) & 1)) * LANES, LANES)]
            side = slot & 1
            block = jnp.where(side == (e & 1), block, pltpu.roll(block, BS, 1))
            out[at, :] = jnp.where(half == side, block, out[at, :])

    out[pl.ds(0, 1), :] = row
    for c in range(6):
        for b in range(2):
            mask = jnp.where(lane < BS, flags[b, 2 * c].astype(F32), flags[b, 2 * c + 1].astype(F32))
            out[pl.ds(1 + c * 2 + b, 1), :] = mask
    out[pl.ds(13, 3), :] = jnp.zeros((3, LANES), F32)


def prepare(left, left_flags, right, right_flags):
    smem = pl.BlockSpec(memory_space=pltpu.SMEM)
    vmem = pl.BlockSpec(memory_space=pltpu.VMEM)
    return pl.pallas_call(
        prepare_kernel,
        out_shape=(jax.ShapeDtypeStruct(left.shape, F32), jax.ShapeDtypeStruct((PACKED, LANES), F32)),
        in_specs=[smem, vmem, smem, vmem],
        out_specs=(vmem, vmem),
        scratch_shapes=[pltpu.SMEM((MAIN + 1,), jnp.int32)],
    )(left_flags, left, right_flags, right)


def split(x):
    high = x.astype(BF)
    return high, (x - high.astype(F32)).astype(BF)


def product_kernel(side, first, last, where, packed, *refs):
    steps = range(first, last)
    count = sum(2 if k == 7 else 1 for k in steps)
    parts, refs = refs[:count], refs[count:]
    if first:
        before, refs = refs[0], refs[1:]
    out, tiles, lefts, high0, high1, low0, low1, homes, tile_sems, left_sems, home_sem = refs
    need = tiles.shape[2]
    copies = {}
    if first:
        sum_copy = pltpu.make_async_copy(before, out, home_sem)
        sum_copy.start()
    if side:
        home_copy = pltpu.make_async_copy(packed.at[:, pl.ds(0, 1), :], homes, home_sem)
        home_copy.start()
    for k in steps:
        n = k - first
        tile = pltpu.make_async_copy(packed.at[pl.ds(where[k] * 2, 2), pl.ds(0, need), :], tiles.at[n], tile_sems.at[n])
        tile.start()
        if k < 7:
            pieces = [pltpu.make_async_copy(parts[n], lefts.at[n], left_sems.at[n])]
        else:
            pieces = [
                pltpu.make_async_copy(parts[n + h], lefts.at[n, pl.ds(h * 256, 256)], left_sems.at[n + h]) for h in range(2)
            ]
        for piece in pieces:
            piece.start()
        copies[k] = [tile] + pieces
    half = lane_half()
    if side:
        home_copy.wait()

    def unpack(k):
        n = k - first
        high, low = (high0, low0) if n % 2 == 0 else (high1, low1)
        for z in range(2):
            for b in range(2):
                for c in range(4):
                    pair = 4 * side + c
                    if pair < 6:
                        mask = tiles[n, z, pl.ds(1 + pair * 2 + b, 1), :]
                        value = tiles[n, z, pl.ds(META + pair * LANES + b * BS, BS), :] * mask
                    else:
                        halves = []
                        for h in range(2):
                            slot = homes[where[k] * 2 + z, 0, b * 4 + 2 * (pair - 6) + h].astype(jnp.int32)
                            kept = slot >= 0
                            slot = jnp.maximum(slot, 0)
                            block = tiles[n, z, pl.ds(pl.multiple_of(META + (slot >> 1) * BS, 16), BS), :]
                            block = jnp.where((slot & 1) == h, block, pltpu.roll(block, BS, 1))
                            halves.append(jnp.where(kept, block, 0.0))
                        value = jnp.where(half == 0, halves[0], halves[1])
                    at = (pl.ds(z * LANES + b * BS, BS), pl.ds(c * LANES, LANES))
                    high[at], low[at] = split(value)
        return high, low

    for k in steps:
        for copy in copies[k]:
            copy.wait()
        high, low = unpack(k)
        left_high, left_low = split(lefts[k - first])
        total = jnp.dot(left_low, high[...], preferred_element_type=F32)
        total += jnp.dot(left_high, low[...], preferred_element_type=F32)
        total += jnp.dot(left_high, high[...], preferred_element_type=F32)
        if k == first and first:
            sum_copy.wait()
        if k:
            total += out[...]
        out[...] = total


def product(side, first, last, parts, where, packed, *before):
    smem = pl.BlockSpec(memory_space=pltpu.SMEM)
    hbm = pl.BlockSpec(memory_space=pltpu.HBM)
    vmem = pl.BlockSpec(memory_space=pltpu.VMEM)
    need = PACKED if side else META + 4 * LANES
    steps = last - first
    half = pltpu.VMEM((256, 512), BF)
    return pl.pallas_call(
        functools.partial(product_kernel, side, first, last),
        out_shape=jax.ShapeDtypeStruct((512, 512), F32),
        in_specs=[smem] + [hbm] * (1 + len(parts)) + [hbm] * len(before),
        out_specs=vmem,
        scratch_shapes=[
            pltpu.VMEM((steps, 2, need, LANES), F32),
            pltpu.VMEM((steps, 512, 256), F32),
            half,
            half,
            half,
            half,
            pltpu.SMEM((16, 1, LANES), F32),
            pltpu.SemaphoreType.DMA((steps,)),
            pltpu.SemaphoreType.DMA((steps + 1,)),
            pltpu.SemaphoreType.DMA,
        ],
        cost_estimate=pl.CostEstimate(flops=6 * 512 * 512 * 256 * steps, bytes_accessed=steps << 20, transcendentals=0),
        compiler_params=pltpu.CompilerParams(vmem_limit_bytes=56 << 20),
    )(where, packed, *parts, *before)


def finish_kernel(where, flags, summed, terms, square, out):
    for b in range(2):
        for c in range(8):
            at = (pl.ds(b * BS, BS), pl.ds(c * LANES, LANES))
            near = (pl.ds(b * BS, BS), pl.ds(c % 4 * LANES, LANES))
            if c < 4:
                total = summed[near]
            else:
                total = (terms[(0,) + near] + terms[(1,) + near]) + (terms[(2,) + near] + terms[(3,) + near])
            line = where[0] * 2 + b
            mask = pair_mask(flags[line, 2 * c], flags[line, 2 * c + 1])
            out[at] = mask * (3.0 * square[at] - 2.0 * total)


def finish(summed, terms, square, flags, where):
    smem = pl.BlockSpec(memory_space=pltpu.SMEM)
    vmem = pl.BlockSpec(memory_space=pltpu.VMEM)
    return pl.pallas_call(
        finish_kernel,
        out_shape=jax.ShapeDtypeStruct(square.shape, F32),
        in_specs=[smem, smem, vmem, vmem, vmem],
        out_specs=vmem,
        cost_estimate=pl.CostEstimate(flops=1 << 20, bytes_accessed=2 << 20, transcendentals=0),
        compiler_params=pltpu.CompilerParams(vmem_limit_bytes=56 << 20),
    )(where, flags, summed, terms, square)


def shift(n, by):
    return [(i, (i + by) % n) for i in range(n)]


def gather_left(own):
    def send(x, by):
        return lax.ppermute(x, "col", shift(8, by))

    up1, down1 = send(own, 1), send(own, -1)
    up2, down2 = send(up1, 1), send(down1, -1)
    up3, down3 = send(up2, 1), send(down2, -1)
    far_a, far_b = send(up3[:256], 1), send(down3[256:], -1)
    return [own, up1, down1, up2, down2, up3, down3, far_a, far_b]


def local(left_slab, right_window, left_pattern, right_pattern, square_blocks, result_pattern):
    left, packed = prepare(left_slab[0], left_pattern[0].T, right_window[0], right_pattern[0])
    packed = lax.all_gather(packed, "row", axis=0, tiled=False)
    parts = gather_left(left)
    me = lax.axis_index("col")
    where = lax.rem(me + jnp.array([8, 7, 9, 6, 10, 5, 11, 12], jnp.int32), 8)
    layer = lax.axis_index("layer").reshape((1,))
    cube = product(0, 0, 7, parts[:7], where, packed)
    cube = product(0, 7, 8, parts[7:], where, packed, cube)
    summed = lax.psum_scatter(cube, "layer", scatter_dimension=0, tiled=True)
    cube = product(1, 0, 8, parts, where, packed)
    terms = lax.all_to_all(cube.reshape(4, 128, 512), "layer", 0, 0)
    return finish(summed, terms, square_blocks, result_pattern, layer)


def solution(mesh):
    in_specs = (
        P("layer", "row", "col"),
        P("layer", "row", "col"),
        P("layer", "row", "col"),
        P("layer", "row", "col"),
        P(("row", "layer"), "col"),
        P("row", "col"),
    )
    out_specs = P(("row", "layer"), "col")
    return jax.shard_map(local, mesh=mesh, in_specs=in_specs, out_specs=out_specs, check_vma=False)
```

```python
import functools

import jax
import jax.numpy as jnp
from jax import lax
from jax.experimental import pallas as pl
from jax.experimental.pallas import tpu as pltpu
from jax.sharding import PartitionSpec as P

BS = 64
LANES = 128
MAIN = 24
EXTRA = 8
META = 16
PACKED = META + 6 * LANES
BF = jnp.bfloat16
F32 = jnp.float32


def lane_half():
    return lax.broadcasted_iota(jnp.int32, (BS, LANES), 1) // BS


def pair_mask(low, high):
    return jnp.where(lane_half() == 0, low.astype(F32), high.astype(F32))


def prepare_kernel(left_flags, left, flags, x, left_out, out, holes):
    for i in range(8):
        for c in range(2):
            mask = pair_mask(left_flags[2 * c, i], left_flags[2 * c + 1, i])
            at = (pl.ds(i * BS, BS), pl.ds(c * LANES, LANES))
            left_out[at] = left[at] * mask
    for c in range(6):
        out[pl.ds(META + c * LANES, LANES), :] = x[:, pl.ds(c * LANES, LANES)]
    count = jnp.int32(0)
    for s in range(MAIN):
        holes[count] = s
        count = count + jnp.where(flags[(s >> 1) & 1, 2 * (s >> 2) + (s & 1)] == 0, 1, 0)
    used = jnp.int32(0)
    half = lane_half()
    lane = lax.broadcasted_iota(jnp.int32, (1, LANES), 1)
    row = jnp.zeros((1, LANES), F32)
    for e in range(EXTRA):
        kept = flags[e >> 2, 12 + (e & 3)] != 0
        slot = holes[jnp.minimum(used, EXTRA)]
        row = jnp.where(lane == e, jnp.where(kept, slot, -1).astype(F32), row)
        used = used + jnp.where(kept, 1, 0)

        @pl.when(kept)
        def _():
            at = pl.ds(pl.multiple_of(META + (slot >> 1) * BS, 16), BS)
            block = x[pl.ds((e >> 2) * BS, BS), pl.ds((6 + ((e >> 1) & 1)) * LANES, LANES)]
            side = slot & 1
            block = jnp.where(side == (e & 1), block, pltpu.roll(block, BS, 1))
            out[at, :] = jnp.where(half == side, block, out[at, :])

    out[pl.ds(0, 1), :] = row
    for c in range(6):
        for b in range(2):
            mask = jnp.where(lane < BS, flags[b, 2 * c].astype(F32), flags[b, 2 * c + 1].astype(F32))
            out[pl.ds(1 + c * 2 + b, 1), :] = mask
    out[pl.ds(13, 3), :] = jnp.zeros((3, LANES), F32)


def prepare(left, left_flags, right, right_flags):
    smem = pl.BlockSpec(memory_space=pltpu.SMEM)
    vmem = pl.BlockSpec(memory_space=pltpu.VMEM)
    return pl.pallas_call(
        prepare_kernel,
        out_shape=(jax.ShapeDtypeStruct(left.shape, F32), jax.ShapeDtypeStruct((PACKED, LANES), F32)),
        in_specs=[smem, vmem, smem, vmem],
        out_specs=(vmem, vmem),
        scratch_shapes=[pltpu.SMEM((MAIN + 1,), jnp.int32)],
    )(left_flags, left, right_flags, right)


def split(x):
    high = x.astype(BF)
    return high, (x - high.astype(F32)).astype(BF)


def product_kernel(place, *refs):
    items, lefts_in = refs[:10], refs[10:18]
    out, tiles, lefts, rights, homes, tile_sems, home_sems, left_sems = refs[18:]
    z, core = place[8], place[9]
    other = 1 - core
    toward = 2 * core - 1

    def tile_copy(source, chip, parity):
        return pltpu.make_async_copy(source, tiles.at[chip, parity], tile_sems.at[chip, parity])

    def home_copy(source, chip, parity):
        return pltpu.make_async_copy(source, homes.at[chip, parity], home_sems.at[chip, parity])

    def left_copy(n):
        return pltpu.make_async_copy(lefts_in[n], lefts.at[n], left_sems.at[n])

    own, swapped, rings, trades = items[0], items[1], items[2:6], items[6:10]
    sources = [(own, 0, core), (swapped, 0, other)]
    for s in range(3):
        sources += [(rings[s].at[0], (s + 1) * toward, core), (rings[s].at[1], (s + 1) * toward, other)]
        sources += [(trades[s].at[0], -(s + 1) * toward, other), (trades[s].at[1], -(s + 1) * toward, core)]
    sources += [(rings[3], 4, core), (trades[3], 4, other)]
    for ref, by, parity in sources:
        chip = (z + by + 8) & 7
        home_copy(ref.at[pl.ds(0, 1)], chip, parity).start()
        tile_copy(ref, chip, parity).start()
    for n in range(8):
        left_copy(n).start()
    half = lane_half()

    def unpack(n, slot):
        chip = place[n]
        for parity in range(2):
            tile_copy(own, chip, parity).wait()
            home_copy(own.at[pl.ds(0, 1)], chip, parity).wait()
        for parity in range(2):
            for b in range(2):
                for pair in range(8):
                    if pair < 6:
                        mask = tiles[chip, parity, pl.ds(1 + pair * 2 + b, 1), :]
                        value = tiles[chip, parity, pl.ds(META + pair * LANES + b * BS, BS), :] * mask
                    else:
                        halves = []
                        for h in range(2):
                            home = homes[chip, parity, 0, b * 4 + 2 * (pair - 6) + h].astype(jnp.int32)
                            kept = home >= 0
                            home = jnp.maximum(home, 0)
                            block = tiles[chip, parity, pl.ds(pl.multiple_of(META + (home >> 1) * BS, 16), BS), :]
                            block = jnp.where((home & 1) == h, block, pltpu.roll(block, BS, 1))
                            halves.append(jnp.where(kept, block, 0.0))
                        value = jnp.where(half == 0, halves[0], halves[1])
                    high, low = split(value)
                    row, columns = parity * LANES + b * BS, pl.ds(pair * LANES, LANES)
                    rights[slot, pl.ds(row, BS), columns] = high
                    rights[slot, pl.ds(256 + row, BS), columns] = high
                    rights[slot, pl.ds(512 + row, BS), columns] = low

    def multiply(n, slot):
        high, low = split(lefts[n])
        left = jnp.concatenate([low, high, high], 1)
        out[...] += jnp.dot(left, rights[slot], preferred_element_type=F32)

    out[...] = jnp.zeros_like(out)
    unpack(0, 0)

    @pl.loop(0, 3)
    def _(i):
        n = 2 * i
        pltpu.make_async_copy(lefts_in[0], lefts.at[n], left_sems.at[n]).wait()
        unpack(n + 1, 1)
        multiply(n, 0)
        pltpu.make_async_copy(lefts_in[0], lefts.at[n + 1], left_sems.at[n + 1]).wait()
        unpack(n + 2, 0)
        multiply(n + 1, 1)

    left_copy(6).wait()
    unpack(7, 1)
    multiply(6, 0)
    left_copy(7).wait()
    multiply(7, 1)


def product(place, items, parts):
    smem = pl.BlockSpec(memory_space=pltpu.SMEM)
    hbm = pl.BlockSpec(memory_space=pltpu.HBM)
    return pl.pallas_call(
        product_kernel,
        out_shape=jax.ShapeDtypeStruct((512, 1024), F32),
        in_specs=[smem] + [hbm] * 18,
        out_specs=pl.BlockSpec(memory_space=pltpu.VMEM),
        scratch_shapes=[
            pltpu.VMEM((8, 2, PACKED, LANES), F32),
            pltpu.VMEM((8, 512, 256), F32),
            pltpu.VMEM((2, 768, 1024), BF),
            pltpu.SMEM((8, 2, 1, LANES), F32),
            pltpu.SemaphoreType.DMA((8, 2)),
            pltpu.SemaphoreType.DMA((8, 2)),
            pltpu.SemaphoreType.DMA((8,)),
        ],
        cost_estimate=pl.CostEstimate(flops=6 * 512 * 1024 * 2048, bytes_accessed=13 << 20, transcendentals=0),
        compiler_params=pltpu.CompilerParams(vmem_limit_bytes=56 << 20),
    )(place, *items, *parts)


def finish_kernel(place, flags, terms, square, out):
    for b in range(2):
        for c in range(8):
            at = (pl.ds(b * BS, BS), pl.ds(c * LANES, LANES))
            total = (terms[(0,) + at] + terms[(1,) + at]) + (terms[(2,) + at] + terms[(3,) + at])
            line = place[10] * 2 + b
            mask = pair_mask(flags[line, 2 * c], flags[line, 2 * c + 1])
            out[at] = mask * (3.0 * square[at] - 2.0 * total)


def finish(place, terms, square, flags):
    smem = pl.BlockSpec(memory_space=pltpu.SMEM)
    vmem = pl.BlockSpec(memory_space=pltpu.VMEM)
    return pl.pallas_call(
        finish_kernel,
        out_shape=jax.ShapeDtypeStruct(square.shape, F32),
        in_specs=[smem, smem, vmem, vmem],
        out_specs=vmem,
        cost_estimate=pl.CostEstimate(flops=1 << 20, bytes_accessed=3 << 20, transcendentals=0),
        compiler_params=pltpu.CompilerParams(vmem_limit_bytes=56 << 20),
    )(place, flags, terms, square)


def shift(n, by):
    return [(i, (i + by) % n) for i in range(n)]


def gather(left, right):
    def send(x, by):
        return lax.ppermute(x, "col", shift(8, by))

    def tie(x, *others):
        return lax.optimization_barrier((x,) + others)[0]

    ring = [(2 * z + c, 2 * ((z + 1 - 2 * c) % 8) + c) for z in range(8) for c in range(2)]
    trade = [(i, i ^ 1) for i in range(16)]
    up = down = left
    parts, rings, trades = [left], [], []
    swapped = lax.ppermute(right, "row", trade)
    pair = jnp.stack([right, swapped])
    for step in range(4):
        up = send(up, 1)
        parts.append(up)
        if step:
            pair = tie(pair, parts[2 * step - 1], down)
        pair = lax.ppermute(pair if step < 3 else pair[0], "row", ring)
        rings.append(pair)
        if step < 3:
            down = send(down, -1)
            parts.append(down)
        trades.append(lax.ppermute(tie(pair, up), "row", trade))
    return [right, swapped] + rings + trades, parts


def local(left_slab, right_window, left_pattern, right_pattern, square_blocks, result_pattern):
    left, packed = prepare(left_slab[0], left_pattern[0].T, right_window[0], right_pattern[0])
    items, parts = gather(left, packed)
    row, col, layer = (lax.axis_index(name) for name in ("row", "col", "layer"))
    arrivals = lax.rem(col + jnp.array([8, 7, 9, 6, 10, 5, 11, 4], jnp.int32), 8)
    place = jnp.concatenate([arrivals, jnp.stack([row >> 1, row & 1, layer])])
    cube = product(place, items, parts)
    terms = lax.all_to_all(cube.reshape(4, 128, 1024), "layer", 0, 0)
    return finish(place, terms, square_blocks, result_pattern)


def solution(mesh):
    in_specs = (
        P("layer", "row", "col"),
        P("layer", "row", "col"),
        P("layer", "row", "col"),
        P("layer", "row", "col"),
        P(("row", "layer"), "col"),
        P("row", "col"),
    )
    out_specs = P(("row", "layer"), "col")
    return jax.shard_map(local, mesh=mesh, in_specs=in_specs, out_specs=out_specs, check_vma=False)
```

```python
import functools

import jax
import jax.numpy as jnp
from jax import lax
from jax.experimental import pallas as pl
from jax.experimental.pallas import tpu as pltpu
from jax.sharding import PartitionSpec as P

BS = 64
LANES = 128
MAIN = 24
EXTRA = 8
META = 16
PACKED = META + 6 * LANES
BF = jnp.bfloat16
F32 = jnp.float32


def lane_half():
    return lax.broadcasted_iota(jnp.int32, (BS, LANES), 1) // BS


def pair_mask(low, high):
    return jnp.where(lane_half() == 0, low.astype(F32), high.astype(F32))


def prepare_kernel(left_flags, left, flags, x, left_out, out, holes):
    for i in range(8):
        for c in range(2):
            mask = pair_mask(left_flags[2 * c, i], left_flags[2 * c + 1, i])
            at = (pl.ds(i * BS, BS), pl.ds(c * LANES, LANES))
            left_out[at] = left[at] * mask
    for c in range(6):
        out[pl.ds(META + c * LANES, LANES), :] = x[:, pl.ds(c * LANES, LANES)]
    count = jnp.int32(0)
    for s in range(MAIN):
        holes[count] = s
        count = count + jnp.where(flags[(s >> 1) & 1, 2 * (s >> 2) + (s & 1)] == 0, 1, 0)
    used = jnp.int32(0)
    half = lane_half()
    lane = lax.broadcasted_iota(jnp.int32, (1, LANES), 1)
    row = jnp.zeros((1, LANES), F32)
    for e in range(EXTRA):
        kept = flags[e >> 2, 12 + (e & 3)] != 0
        slot = holes[jnp.minimum(used, EXTRA)]
        row = jnp.where(lane == e, jnp.where(kept, slot, -1).astype(F32), row)
        used = used + jnp.where(kept, 1, 0)

        @pl.when(kept)
        def _():
            at = pl.ds(pl.multiple_of(META + (slot >> 1) * BS, 16), BS)
            block = x[pl.ds((e >> 2) * BS, BS), pl.ds((6 + ((e >> 1) & 1)) * LANES, LANES)]
            side = slot & 1
            block = jnp.where(side == (e & 1), block, pltpu.roll(block, BS, 1))
            out[at, :] = jnp.where(half == side, block, out[at, :])

    out[pl.ds(0, 1), :] = row
    for c in range(6):
        for b in range(2):
            mask = jnp.where(lane < BS, flags[b, 2 * c].astype(F32), flags[b, 2 * c + 1].astype(F32))
            out[pl.ds(1 + c * 2 + b, 1), :] = mask
    out[pl.ds(13, 3), :] = jnp.zeros((3, LANES), F32)


def prepare(left, left_flags, right, right_flags):
    smem = pl.BlockSpec(memory_space=pltpu.SMEM)
    vmem = pl.BlockSpec(memory_space=pltpu.VMEM)
    return pl.pallas_call(
        prepare_kernel,
        out_shape=(jax.ShapeDtypeStruct(left.shape, F32), jax.ShapeDtypeStruct((PACKED, LANES), F32)),
        in_specs=[smem, vmem, smem, vmem],
        out_specs=(vmem, vmem),
        scratch_shapes=[pltpu.SMEM((MAIN + 1,), jnp.int32)],
    )(left_flags, left, right_flags, right)


def split(x):
    high = x.astype(BF)
    return high, (x - high.astype(F32)).astype(BF)


def product_kernel(side, place, left, *refs):
    items = refs[:10]
    out, tiles, lefts, rights, homes, tile_sems, home_sems, left_sems = refs[10:]
    need = tiles.shape[2]
    z, core = place[0], place[1]
    other = 1 - core
    toward = 2 * core - 1

    def tile_copy(source, n, parity):
        return pltpu.make_async_copy(source.at[pl.ds(0, need)], tiles.at[n, parity], tile_sems.at[n, parity])

    def home_copy(source, n, parity):
        return pltpu.make_async_copy(source.at[pl.ds(0, 1)], homes.at[n, parity], home_sems.at[n, parity])

    def left_copy(n, chip):
        return pltpu.make_async_copy(left.at[chip], lefts.at[n], left_sems.at[n])

    own, swapped, rings, trades = items[0], items[1], items[2:6], items[6:10]
    chunks = [(0, (own, core), (swapped, other))]
    for s in range(3):
        chunks.append(((s + 1) * toward, (rings[s].at[0], core), (rings[s].at[1], other)))
        chunks.append((-(s + 1) * toward, (trades[s].at[0], other), (trades[s].at[1], core)))
    chunks.append((4, (rings[3], core), (trades[3], other)))
    for n, (by, *pieces) in enumerate(chunks):
        for ref, parity in pieces:
            if side:
                home_copy(ref, n, parity).start()
            tile_copy(ref, n, parity).start()
        left_copy(n, (z + by + 8) & 7).start()
    half = lane_half()

    def unpack(n, slot):
        for parity in range(2):
            tile_copy(own, n, parity).wait()
            if side:
                home_copy(own, n, parity).wait()
        for parity in range(2):
            for b in range(2):
                for c in range(4):
                    pair = 4 * side + c
                    if pair < 6:
                        mask = tiles[n, parity, pl.ds(1 + pair * 2 + b, 1), :]
                        value = tiles[n, parity, pl.ds(META + pair * LANES + b * BS, BS), :] * mask
                    else:
                        halves = []
                        for h in range(2):
                            home = homes[n, parity, 0, b * 4 + 2 * (pair - 6) + h].astype(jnp.int32)
                            kept = home >= 0
                            home = jnp.maximum(home, 0)
                            block = tiles[n, parity, pl.ds(pl.multiple_of(META + (home >> 1) * BS, 16), BS), :]
                            block = jnp.where((home & 1) == h, block, pltpu.roll(block, BS, 1))
                            halves.append(jnp.where(kept, block, 0.0))
                        value = jnp.where(half == 0, halves[0], halves[1])
                    high, low = split(value)
                    row, columns = parity * LANES + b * BS, pl.ds(c * LANES, LANES)
                    rights[slot, pl.ds(row, BS), columns] = high
                    rights[slot, pl.ds(256 + row, BS), columns] = high
                    rights[slot, pl.ds(512 + row, BS), columns] = low

    def multiply(n, slot):
        high, low = split(lefts[n])
        return jnp.dot(jnp.concatenate([low, high, high], 1), rights[slot], preferred_element_type=F32)

    unpack(0, 0)
    for n in range(8):
        left_copy(n, 0).wait()
        if n < 7:
            unpack(n + 1, (n + 1) % 2)
        total = multiply(n, n % 2)
        out[...] = total + out[...] if n else total


def product(side, place, left, items):
    smem = pl.BlockSpec(memory_space=pltpu.SMEM)
    hbm = pl.BlockSpec(memory_space=pltpu.HBM)
    need = PACKED if side else META + 4 * LANES
    return pl.pallas_call(
        functools.partial(product_kernel, side),
        out_shape=jax.ShapeDtypeStruct((512, 512), F32),
        in_specs=[smem] + [hbm] * 11,
        out_specs=pl.BlockSpec(memory_space=pltpu.VMEM),
        scratch_shapes=[
            pltpu.VMEM((8, 2, need, LANES), F32),
            pltpu.VMEM((8, 512, 256), F32),
            pltpu.VMEM((2, 768, 512), BF),
            pltpu.SMEM((8, 2, 1, LANES), F32),
            pltpu.SemaphoreType.DMA((8, 2)),
            pltpu.SemaphoreType.DMA((8, 2)),
            pltpu.SemaphoreType.DMA((8,)),
        ],
        cost_estimate=pl.CostEstimate(flops=6 * 512 * 512 * 2048, bytes_accessed=10 << 20, transcendentals=0),
        compiler_params=pltpu.CompilerParams(vmem_limit_bytes=56 << 20),
    )(place, left, *items)


def finish_kernel(side, place, flags, terms, square, *refs):
    out = refs[-1]
    for b in range(2):
        for c in range(4):
            at = (pl.ds(b * BS, BS), pl.ds(c * LANES, LANES))
            total = (terms[(0,) + at] + terms[(1,) + at]) + (terms[(2,) + at] + terms[(3,) + at])
            line, column = place[2] * 2 + b, 8 * side + 2 * c
            mask = pair_mask(flags[line, column], flags[line, column + 1])
            out[at] = mask * (3.0 * square[at] - 2.0 * total)


def finish(side, terms, square, flags, place, *before):
    smem = pl.BlockSpec(memory_space=pltpu.SMEM)
    half = pl.BlockSpec((128, 512), lambda i: (0, side))
    return pl.pallas_call(
        functools.partial(finish_kernel, side),
        out_shape=jax.ShapeDtypeStruct(square.shape, F32),
        grid=(1,),
        in_specs=[smem, smem, pl.BlockSpec((4, 128, 512), lambda i: (0, 0, 0)), half]
        + [pl.BlockSpec(memory_space=pltpu.HBM)] * len(before),
        out_specs=half,
        input_output_aliases={4: 0} if before else {},
        cost_estimate=pl.CostEstimate(flops=1 << 20, bytes_accessed=2 << 20, transcendentals=0),
        compiler_params=pltpu.CompilerParams(vmem_limit_bytes=56 << 20),
    )(place, flags, terms, square, *before)


def gather_right(own):
    ring = [(2 * z + c, 2 * ((z + 1 - 2 * c) % 8) + c) for z in range(8) for c in range(2)]
    trade = [(i, i ^ 1) for i in range(16)]
    swapped = lax.ppermute(own, "row", trade)
    rings, pair = [], jnp.stack([own, swapped])
    for step in range(4):
        pair = lax.ppermute(pair if step < 3 else pair[0], "row", ring)
        rings.append(pair)
    return [own, swapped] + rings + [lax.ppermute(pair, "row", trade) for pair in rings]


def local(left_slab, right_window, left_pattern, right_pattern, square_blocks, result_pattern):
    left, packed = prepare(left_slab[0], left_pattern[0].T, right_window[0], right_pattern[0])
    left = lax.all_gather(left, "col", axis=0, tiled=False)
    items = gather_right(packed)
    row, layer = lax.axis_index("row"), lax.axis_index("layer")
    place = jnp.stack([row >> 1, row & 1, layer])
    out = ()
    for side in range(2):
        cube = product(side, place, left, items)
        terms = lax.all_to_all(cube.reshape(4, 128, 512), "layer", 0, 0)
        out = (finish(side, terms, square_blocks, result_pattern, place, *out),)
    return out[0]


def solution(mesh):
    in_specs = (
        P("layer", "row", "col"),
        P("layer", "row", "col"),
        P("layer", "row", "col"),
        P("layer", "row", "col"),
        P(("row", "layer"), "col"),
        P("row", "col"),
    )
    out_specs = P(("row", "layer"), "col")
    return jax.shard_map(local, mesh=mesh, in_specs=in_specs, out_specs=out_specs, check_vma=False)
```

```python
import functools

import jax
import jax.numpy as jnp
from jax import lax
from jax.experimental import pallas as pl
from jax.experimental.pallas import tpu as pltpu
from jax.sharding import PartitionSpec as P

BS = 64
LANES = 128
MAIN = 24
EXTRA = 8
META = 16
PACKED = META + 6 * LANES
BF = jnp.bfloat16
F32 = jnp.float32


def lane_half():
    return lax.broadcasted_iota(jnp.int32, (BS, LANES), 1) // BS


def pair_mask(low, high):
    return jnp.where(lane_half() == 0, low.astype(F32), high.astype(F32))


def prepare_kernel(left_flags, left, flags, x, left_out, out, holes):
    for i in range(8):
        for c in range(2):
            mask = pair_mask(left_flags[2 * c, i], left_flags[2 * c + 1, i])
            at = (pl.ds(i * BS, BS), pl.ds(c * LANES, LANES))
            left_out[at] = left[at] * mask
    for c in range(6):
        out[pl.ds(META + c * LANES, LANES), :] = x[:, pl.ds(c * LANES, LANES)]
    count = jnp.int32(0)
    for s in range(MAIN):
        holes[count] = s
        count = count + jnp.where(flags[(s >> 1) & 1, 2 * (s >> 2) + (s & 1)] == 0, 1, 0)
    used = jnp.int32(0)
    half = lane_half()
    lane = lax.broadcasted_iota(jnp.int32, (1, LANES), 1)
    row = jnp.zeros((1, LANES), F32)
    for e in range(EXTRA):
        kept = flags[e >> 2, 12 + (e & 3)] != 0
        slot = holes[jnp.minimum(used, EXTRA)]
        row = jnp.where(lane == e, jnp.where(kept, slot, -1).astype(F32), row)
        used = used + jnp.where(kept, 1, 0)

        @pl.when(kept)
        def _():
            at = pl.ds(pl.multiple_of(META + (slot >> 1) * BS, 16), BS)
            block = x[pl.ds((e >> 2) * BS, BS), pl.ds((6 + ((e >> 1) & 1)) * LANES, LANES)]
            side = slot & 1
            block = jnp.where(side == (e & 1), block, pltpu.roll(block, BS, 1))
            out[at, :] = jnp.where(half == side, block, out[at, :])

    out[pl.ds(0, 1), :] = row
    for c in range(6):
        for b in range(2):
            mask = jnp.where(lane < BS, flags[b, 2 * c].astype(F32), flags[b, 2 * c + 1].astype(F32))
            out[pl.ds(1 + c * 2 + b, 1), :] = mask
    out[pl.ds(13, 3), :] = jnp.zeros((3, LANES), F32)


def prepare(left, left_flags, right, right_flags):
    smem = pl.BlockSpec(memory_space=pltpu.SMEM)
    vmem = pl.BlockSpec(memory_space=pltpu.VMEM)
    return pl.pallas_call(
        prepare_kernel,
        out_shape=(jax.ShapeDtypeStruct(left.shape, F32), jax.ShapeDtypeStruct((PACKED, LANES), F32)),
        in_specs=[smem, vmem, smem, vmem],
        out_specs=(vmem, vmem),
        scratch_shapes=[pltpu.SMEM((MAIN + 1,), jnp.int32)],
    )(left_flags, left, right_flags, right)


def split(x):
    high = x.astype(BF)
    return high, (x - high.astype(F32)).astype(BF)


def product_kernel(side, place, left, *refs):
    items = refs[:16]
    out, tiles, lefts, rights, homes, tile_sems, home_sems, left_sems = refs[16:]
    need = tiles.shape[2]
    z, core = place[0], place[1]
    other = 1 - core

    def tile_copy(source, n, parity):
        return pltpu.make_async_copy(source.at[pl.ds(0, need)], tiles.at[n, parity], tile_sems.at[n, parity])

    def home_copy(source, n, parity):
        return pltpu.make_async_copy(source.at[pl.ds(0, 1)], homes.at[n, parity], home_sems.at[n, parity])

    def left_copy(n, chip):
        return pltpu.make_async_copy(left.at[chip], lefts.at[n], left_sems.at[n])

    chunks = [(by, (items[2 * n], core), (items[2 * n + 1], other)) for n, by in enumerate((0, -1, 1, -2, 2, -3, 3, 4))]
    for n, (by, *pieces) in enumerate(chunks):
        for ref, parity in pieces:
            if side:
                home_copy(ref, n, parity).start()
            tile_copy(ref, n, parity).start()
        left_copy(n, (z + by + 8) & 7).start()
    half = lane_half()

    def unpack(n, slot):
        for parity in range(2):
            tile_copy(items[0], n, parity).wait()
            if side:
                home_copy(items[0], n, parity).wait()
        for parity in range(2):
            for b in range(2):
                for c in range(4):
                    pair = 4 * side + c
                    if pair < 6:
                        mask = tiles[n, parity, pl.ds(1 + pair * 2 + b, 1), :]
                        value = tiles[n, parity, pl.ds(META + pair * LANES + b * BS, BS), :] * mask
                    else:
                        halves = []
                        for h in range(2):
                            home = homes[n, parity, 0, b * 4 + 2 * (pair - 6) + h].astype(jnp.int32)
                            kept = home >= 0
                            home = jnp.maximum(home, 0)
                            block = tiles[n, parity, pl.ds(pl.multiple_of(META + (home >> 1) * BS, 16), BS), :]
                            block = jnp.where((home & 1) == h, block, pltpu.roll(block, BS, 1))
                            halves.append(jnp.where(kept, block, 0.0))
                        value = jnp.where(half == 0, halves[0], halves[1])
                    high, low = split(value)
                    row, columns = parity * LANES + b * BS, pl.ds(c * LANES, LANES)
                    rights[slot, pl.ds(row, BS), columns] = high
                    rights[slot, pl.ds(256 + row, BS), columns] = high
                    rights[slot, pl.ds(512 + row, BS), columns] = low

    def multiply(n, slot):
        high, low = split(lefts[n])
        return jnp.dot(jnp.concatenate([low, high, high], 1), rights[slot], preferred_element_type=F32)

    unpack(0, 0)
    for n in range(8):
        left_copy(n, 0).wait()
        if n < 7:
            unpack(n + 1, (n + 1) % 2)
        total = multiply(n, n % 2)
        out[...] = total + out[...] if n else total


def product(side, place, left, items):
    smem = pl.BlockSpec(memory_space=pltpu.SMEM)
    hbm = pl.BlockSpec(memory_space=pltpu.HBM)
    need = PACKED if side else META + 4 * LANES
    return pl.pallas_call(
        functools.partial(product_kernel, side),
        out_shape=jax.ShapeDtypeStruct((512, 512), F32),
        in_specs=[smem] + [hbm] * 17,
        out_specs=pl.BlockSpec(memory_space=pltpu.VMEM),
        scratch_shapes=[
            pltpu.VMEM((8, 2, need, LANES), F32),
            pltpu.VMEM((8, 512, 256), F32),
            pltpu.VMEM((2, 768, 512), BF),
            pltpu.SMEM((8, 2, 1, LANES), F32),
            pltpu.SemaphoreType.DMA((8, 2)),
            pltpu.SemaphoreType.DMA((8, 2)),
            pltpu.SemaphoreType.DMA((8,)),
        ],
        cost_estimate=pl.CostEstimate(flops=6 * 512 * 512 * 2048, bytes_accessed=10 << 20, transcendentals=0),
        compiler_params=pltpu.CompilerParams(vmem_limit_bytes=56 << 20),
    )(place, left, *items)


def finish_kernel(side, place, flags, terms_in, square, *refs):
    out, terms, sems = refs[-3:]
    copies = [pltpu.make_async_copy(terms_in.at[n], terms.at[n], sems.at[n]) for n in range(4)]
    for copy in copies:
        copy.start()
    for copy in copies:
        copy.wait()
    for b in range(2):
        for c in range(4):
            at = (pl.ds(b * BS, BS), pl.ds(c * LANES, LANES))
            total = (terms[(0,) + at] + terms[(1,) + at]) + (terms[(2,) + at] + terms[(3,) + at])
            line, column = place[2] * 2 + b, 8 * side + 2 * c
            mask = pair_mask(flags[line, column], flags[line, column + 1])
            out[at] = mask * (3.0 * square[at] - 2.0 * total)


def finish(side, terms, square, flags, place, *before):
    smem = pl.BlockSpec(memory_space=pltpu.SMEM)
    hbm = pl.BlockSpec(memory_space=pltpu.HBM)
    half = pl.BlockSpec((128, 512), lambda i: (0, side))
    return pl.pallas_call(
        functools.partial(finish_kernel, side),
        out_shape=jax.ShapeDtypeStruct(square.shape, F32),
        grid=(1,),
        in_specs=[smem, smem, hbm, half] + [hbm] * len(before),
        out_specs=half,
        scratch_shapes=[pltpu.VMEM((4, 128, 512), F32), pltpu.SemaphoreType.DMA((4,))],
        input_output_aliases={4: 0} if before else {},
        cost_estimate=pl.CostEstimate(flops=1 << 20, bytes_accessed=2 << 20, transcendentals=0),
        compiler_params=pltpu.CompilerParams(vmem_limit_bytes=56 << 20),
    )(place, flags, terms, square, *before)


def shift(n, by):
    return [(i, (i + by) % n) for i in range(n)]


def gather_right(own):
    trade = [(i, i ^ 1) for i in range(16)]

    def send(x, by, after):
        x = lax.optimization_barrier((x, *after))[0]
        return lax.ppermute(x, "row", shift(16, 2 * by))

    up = down = own
    arrivals, traded = [own], [lax.ppermute(own, "row", trade)]
    for step in range(4):
        after = traded[:1] if step == 1 else traded[2 * step - 3 : 2 * step - 1] if step else []
        up = send(up, 1, after)
        arrivals.append(up)
        if step < 3:
            down = send(down, -1, after)
            arrivals.append(down)
        traded += [lax.ppermute(x, "row", trade) for x in arrivals[len(traded) :]]
    return [x for both in zip(arrivals, traded) for x in both]


def local(left_slab, right_window, left_pattern, right_pattern, square_blocks, result_pattern):
    left, packed = prepare(left_slab[0], left_pattern[0].T, right_window[0], right_pattern[0])
    left = lax.all_gather(left, "col", axis=0, tiled=False)
    items = gather_right(packed)
    row, layer = lax.axis_index("row"), lax.axis_index("layer")
    place = jnp.stack([row >> 1, row & 1, layer])
    out = ()
    for side in range(2):
        cube = product(side, place, left, items)
        terms = lax.all_to_all(cube.reshape(4, 128, 512), "layer", 0, 0)
        out = (finish(side, terms, square_blocks, result_pattern, place, *out),)
    return out[0]


def solution(mesh):
    in_specs = (
        P("layer", "row", "col"),
        P("layer", "row", "col"),
        P("layer", "row", "col"),
        P("layer", "row", "col"),
        P(("row", "layer"), "col"),
        P("row", "col"),
    )
    out_specs = P(("row", "layer"), "col")
    return jax.shard_map(local, mesh=mesh, in_specs=in_specs, out_specs=out_specs, check_vma=False)
```

```python
import functools

import jax
import jax.numpy as jnp
from jax import lax
from jax.experimental import pallas as pl
from jax.experimental.pallas import tpu as pltpu
from jax.sharding import PartitionSpec as P

BS = 64
LANES = 128
MAIN = 24
EXTRA = 8
META = 16
PACKED = META + 6 * LANES
BF = jnp.bfloat16
F32 = jnp.float32


def lane_half():
    return lax.broadcasted_iota(jnp.int32, (BS, LANES), 1) // BS


def pair_mask(low, high):
    return jnp.where(lane_half() == 0, low.astype(F32), high.astype(F32))


def prepare_kernel(left_flags, left, flags, x, left_out, out, holes):
    for i in range(8):
        for c in range(2):
            mask = pair_mask(left_flags[2 * c, i], left_flags[2 * c + 1, i])
            at = (pl.ds(i * BS, BS), pl.ds(c * LANES, LANES))
            left_out[at] = left[at] * mask
    for c in range(6):
        out[pl.ds(META + c * LANES, LANES), :] = x[:, pl.ds(c * LANES, LANES)]
    count = jnp.int32(0)
    for s in range(MAIN):
        holes[count] = s
        count = count + jnp.where(flags[(s >> 1) & 1, 2 * (s >> 2) + (s & 1)] == 0, 1, 0)
    used = jnp.int32(0)
    half = lane_half()
    lane = lax.broadcasted_iota(jnp.int32, (1, LANES), 1)
    row = jnp.zeros((1, LANES), F32)
    for e in range(EXTRA):
        kept = flags[e >> 2, 12 + (e & 3)] != 0
        slot = holes[jnp.minimum(used, EXTRA)]
        row = jnp.where(lane == e, jnp.where(kept, slot, -1).astype(F32), row)
        used = used + jnp.where(kept, 1, 0)

        @pl.when(kept)
        def _():
            at = pl.ds(pl.multiple_of(META + (slot >> 1) * BS, 16), BS)
            block = x[pl.ds((e >> 2) * BS, BS), pl.ds((6 + ((e >> 1) & 1)) * LANES, LANES)]
            side = slot & 1
            block = jnp.where(side == (e & 1), block, pltpu.roll(block, BS, 1))
            out[at, :] = jnp.where(half == side, block, out[at, :])

    out[pl.ds(0, 1), :] = row
    for c in range(6):
        for b in range(2):
            mask = jnp.where(lane < BS, flags[b, 2 * c].astype(F32), flags[b, 2 * c + 1].astype(F32))
            out[pl.ds(1 + c * 2 + b, 1), :] = mask
    out[pl.ds(13, 3), :] = jnp.zeros((3, LANES), F32)


def prepare(left, left_flags, right, right_flags):
    smem = pl.BlockSpec(memory_space=pltpu.SMEM)
    vmem = pl.BlockSpec(memory_space=pltpu.VMEM)
    return pl.pallas_call(
        prepare_kernel,
        out_shape=(jax.ShapeDtypeStruct(left.shape, F32), jax.ShapeDtypeStruct((PACKED, LANES), F32)),
        in_specs=[smem, vmem, smem, vmem],
        out_specs=(vmem, vmem),
        scratch_shapes=[pltpu.SMEM((MAIN + 1,), jnp.int32)],
    )(left_flags, left, right_flags, right)


def split(x):
    high = x.astype(BF)
    return high, (x - high.astype(F32)).astype(BF)


def product_kernel(side, first, last, where, packed, *refs):
    steps = range(first, last)
    parts, refs = refs[: last - first], refs[last - first :]
    if first:
        before, refs = refs[0], refs[1:]
    out, tiles, lefts, high0, high1, low0, low1, homes, tile_sems, left_sems, home_sem = refs
    need = tiles.shape[2]
    copies = {}
    if first:
        sum_copy = pltpu.make_async_copy(before, out, home_sem)
        sum_copy.start()
    if side:
        home_copy = pltpu.make_async_copy(packed.at[:, pl.ds(0, 1), :], homes, home_sem)
        home_copy.start()
    for k in steps:
        n = k - first
        tile = pltpu.make_async_copy(packed.at[pl.ds(where[k] * 2, 2), pl.ds(0, need), :], tiles.at[n], tile_sems.at[n])
        tile.start()
        part = pltpu.make_async_copy(parts[n], lefts.at[n], left_sems.at[n])
        part.start()
        copies[k] = [tile, part]
    half = lane_half()
    if side:
        home_copy.wait()

    def unpack(k):
        n = k - first
        high, low = (high0, low0) if n % 2 == 0 else (high1, low1)
        for z in range(2):
            for b in range(2):
                for c in range(4):
                    pair = 4 * side + c
                    if pair < 6:
                        mask = tiles[n, z, pl.ds(1 + pair * 2 + b, 1), :]
                        value = tiles[n, z, pl.ds(META + pair * LANES + b * BS, BS), :] * mask
                    else:
                        halves = []
                        for h in range(2):
                            slot = homes[where[k] * 2 + z, 0, b * 4 + 2 * (pair - 6) + h].astype(jnp.int32)
                            kept = slot >= 0
                            slot = jnp.maximum(slot, 0)
                            block = tiles[n, z, pl.ds(pl.multiple_of(META + (slot >> 1) * BS, 16), BS), :]
                            block = jnp.where((slot & 1) == h, block, pltpu.roll(block, BS, 1))
                            halves.append(jnp.where(kept, block, 0.0))
                        value = jnp.where(half == 0, halves[0], halves[1])
                    at = (pl.ds(z * LANES + b * BS, BS), pl.ds(c * LANES, LANES))
                    high[at], low[at] = split(value)
        return high, low

    for k in steps:
        for copy in copies[k]:
            copy.wait()
        high, low = unpack(k)
        left_high, left_low = split(lefts[k - first])
        total = jnp.dot(left_low, high[...], preferred_element_type=F32)
        total += jnp.dot(left_high, low[...], preferred_element_type=F32)
        total += jnp.dot(left_high, high[...], preferred_element_type=F32)
        if k == first and first:
            sum_copy.wait()
        if k:
            total += out[...]
        out[...] = total


def product(side, first, last, parts, where, packed, *before):
    smem = pl.BlockSpec(memory_space=pltpu.SMEM)
    hbm = pl.BlockSpec(memory_space=pltpu.HBM)
    vmem = pl.BlockSpec(memory_space=pltpu.VMEM)
    need = PACKED if side else META + 4 * LANES
    steps = last - first
    half = pltpu.VMEM((256, 512), BF)
    return pl.pallas_call(
        functools.partial(product_kernel, side, first, last),
        out_shape=jax.ShapeDtypeStruct((512, 512), F32),
        in_specs=[smem] + [hbm] * (1 + len(parts)) + [hbm] * len(before),
        out_specs=vmem,
        scratch_shapes=[
            pltpu.VMEM((steps, 2, need, LANES), F32),
            pltpu.VMEM((steps, 512, 256), F32),
            half,
            half,
            half,
            half,
            pltpu.SMEM((16, 1, LANES), F32),
            pltpu.SemaphoreType.DMA((steps,)),
            pltpu.SemaphoreType.DMA((steps,)),
            pltpu.SemaphoreType.DMA,
        ],
        cost_estimate=pl.CostEstimate(flops=6 * 512 * 512 * 256 * steps, bytes_accessed=steps << 20, transcendentals=0),
        compiler_params=pltpu.CompilerParams(vmem_limit_bytes=56 << 20),
    )(where, packed, *parts, *before)


def finish_kernel(side, where, flags, terms, square, *refs):
    out = refs[-1]
    for b in range(2):
        for c in range(4):
            at = (pl.ds(b * BS, BS), pl.ds(c * LANES, LANES))
            total = (terms[(0,) + at] + terms[(1,) + at]) + (terms[(2,) + at] + terms[(3,) + at])
            line, column = where[0] * 2 + b, 8 * side + 2 * c
            mask = pair_mask(flags[line, column], flags[line, column + 1])
            out[at] = mask * (3.0 * square[at] - 2.0 * total)


def finish(side, terms, square, flags, where, *before):
    smem = pl.BlockSpec(memory_space=pltpu.SMEM)
    half = pl.BlockSpec((128, 512), lambda i: (0, side))
    return pl.pallas_call(
        functools.partial(finish_kernel, side),
        out_shape=jax.ShapeDtypeStruct(square.shape, F32),
        grid=(1,),
        in_specs=[smem, smem, pl.BlockSpec((4, 128, 512), lambda i: (0, 0, 0)), half]
        + [pl.BlockSpec(memory_space=pltpu.HBM)] * len(before),
        out_specs=half,
        input_output_aliases={4: 0} if before else {},
        cost_estimate=pl.CostEstimate(flops=1 << 20, bytes_accessed=2 << 20, transcendentals=0),
    )(where, flags, terms, square, *before)


def shift(n, by):
    return [(i, (i + by) % n) for i in range(n)]


def gather_left(own):
    def send(x, by):
        return lax.ppermute(x, "col", shift(8, by))

    up1, down1 = send(own, 1), send(own, -1)
    up2, down2 = send(up1, 1), send(down1, -1)
    up3, down3 = send(up2, 1), send(down2, -1)
    return [own, up1, down1, up2, down2, up3, down3, send(up3, 1)]


def local(left_slab, right_window, left_pattern, right_pattern, square_blocks, result_pattern):
    left, packed = prepare(left_slab[0], left_pattern[0].T, right_window[0], right_pattern[0])
    packed = lax.all_gather(packed, "row", axis=0, tiled=False)
    parts = gather_left(left)
    me = lax.axis_index("col")
    where = lax.rem(me + jnp.array([8, 7, 9, 6, 10, 5, 11, 12], jnp.int32), 8)
    layer = lax.axis_index("layer").reshape((1,))
    out = ()
    for side in range(2):
        if side:
            cube = product(side, 0, 8, parts, where, packed)
        else:
            cube = product(side, 0, 7, parts[:7], where, packed)
            cube = product(side, 7, 8, parts[7:], where, packed, cube)
        terms = lax.all_to_all(cube.reshape(4, 128, 512), "layer", 0, 0)
        out = (finish(side, terms, square_blocks, result_pattern, layer, *out),)
    return out[0]


def solution(mesh):
    in_specs = (
        P("layer", "row", "col"),
        P("layer", "row", "col"),
        P("layer", "row", "col"),
        P("layer", "row", "col"),
        P(("row", "layer"), "col"),
        P("row", "col"),
    )
    out_specs = P(("row", "layer"), "col")
    return jax.shard_map(local, mesh=mesh, in_specs=in_specs, out_specs=out_specs, check_vma=False)
```

```python
import functools

import jax
import jax.numpy as jnp
from jax import lax
from jax.experimental import pallas as pl
from jax.experimental.pallas import tpu as pltpu
from jax.sharding import PartitionSpec as P

BS = 64
LANES = 128
MAIN = 24
EXTRA = 8
META = 16
PACKED = META + 6 * LANES
BF = jnp.bfloat16
F32 = jnp.float32


def lane_half():
    return lax.broadcasted_iota(jnp.int32, (BS, LANES), 1) // BS


def pair_mask(low, high):
    return jnp.where(lane_half() == 0, low.astype(F32), high.astype(F32))


def prepare_kernel(left_flags, left, flags, x, left_out, out, holes):
    for i in range(8):
        for c in range(2):
            mask = pair_mask(left_flags[2 * c, i], left_flags[2 * c + 1, i])
            at = (pl.ds(i * BS, BS), pl.ds(c * LANES, LANES))
            left_out[at] = left[at] * mask
    for c in range(6):
        out[pl.ds(META + c * LANES, LANES), :] = x[:, pl.ds(c * LANES, LANES)]
    count = jnp.int32(0)
    for s in range(MAIN):
        holes[count] = s
        count = count + jnp.where(flags[(s >> 1) & 1, 2 * (s >> 2) + (s & 1)] == 0, 1, 0)
    used = jnp.int32(0)
    half = lane_half()
    lane = lax.broadcasted_iota(jnp.int32, (1, LANES), 1)
    row = jnp.zeros((1, LANES), F32)
    for e in range(EXTRA):
        kept = flags[e >> 2, 12 + (e & 3)] != 0
        slot = holes[jnp.minimum(used, EXTRA)]
        row = jnp.where(lane == e, jnp.where(kept, slot, -1).astype(F32), row)
        used = used + jnp.where(kept, 1, 0)

        @pl.when(kept)
        def _():
            at = pl.ds(pl.multiple_of(META + (slot >> 1) * BS, 16), BS)
            block = x[pl.ds((e >> 2) * BS, BS), pl.ds((6 + ((e >> 1) & 1)) * LANES, LANES)]
            side = slot & 1
            block = jnp.where(side == (e & 1), block, pltpu.roll(block, BS, 1))
            out[at, :] = jnp.where(half == side, block, out[at, :])

    out[pl.ds(0, 1), :] = row
    for c in range(6):
        for b in range(2):
            mask = jnp.where(lane < BS, flags[b, 2 * c].astype(F32), flags[b, 2 * c + 1].astype(F32))
            out[pl.ds(1 + c * 2 + b, 1), :] = mask
    out[pl.ds(13, 3), :] = jnp.zeros((3, LANES), F32)


def prepare(left, left_flags, right, right_flags):
    smem = pl.BlockSpec(memory_space=pltpu.SMEM)
    vmem = pl.BlockSpec(memory_space=pltpu.VMEM)
    return pl.pallas_call(
        prepare_kernel,
        out_shape=(jax.ShapeDtypeStruct(left.shape, F32), jax.ShapeDtypeStruct((PACKED, LANES), F32)),
        in_specs=[smem, vmem, smem, vmem],
        out_specs=(vmem, vmem),
        scratch_shapes=[pltpu.SMEM((MAIN + 1,), jnp.int32)],
    )(left_flags, left, right_flags, right)


def split(x):
    high = x.astype(BF)
    return high, (x - high.astype(F32)).astype(BF)


def product_kernel(side, first, last, where, packed, *refs):
    steps = range(first, last)
    parts, refs = refs[: last - first], refs[last - first :]
    if first:
        before, refs = refs[0], refs[1:]
    out, tiles, lefts, high0, high1, low0, low1, homes, tile_sems, left_sems, home_sem = refs
    need = tiles.shape[2]
    copies = {}
    if first:
        sum_copy = pltpu.make_async_copy(before, out, home_sem)
        sum_copy.start()
    if side:
        home_copy = pltpu.make_async_copy(packed.at[:, pl.ds(0, 1), :], homes, home_sem)
        home_copy.start()
    for k in steps:
        n = k - first
        tile = pltpu.make_async_copy(packed.at[pl.ds(where[k] * 2, 2), pl.ds(0, need), :], tiles.at[n], tile_sems.at[n])
        tile.start()
        part = pltpu.make_async_copy(parts[n], lefts.at[n], left_sems.at[n])
        part.start()
        copies[k] = [tile, part]
    half = lane_half()
    if side:
        home_copy.wait()

    def unpack(k):
        n = k - first
        high, low = (high0, low0) if n % 2 == 0 else (high1, low1)
        for z in range(2):
            for b in range(2):
                for c in range(4):
                    pair = 4 * side + c
                    if pair < 6:
                        mask = tiles[n, z, pl.ds(1 + pair * 2 + b, 1), :]
                        value = tiles[n, z, pl.ds(META + pair * LANES + b * BS, BS), :] * mask
                    else:
                        halves = []
                        for h in range(2):
                            slot = homes[where[k] * 2 + z, 0, b * 4 + 2 * (pair - 6) + h].astype(jnp.int32)
                            kept = slot >= 0
                            slot = jnp.maximum(slot, 0)
                            block = tiles[n, z, pl.ds(pl.multiple_of(META + (slot >> 1) * BS, 16), BS), :]
                            block = jnp.where((slot & 1) == h, block, pltpu.roll(block, BS, 1))
                            halves.append(jnp.where(kept, block, 0.0))
                        value = jnp.where(half == 0, halves[0], halves[1])
                    at = (pl.ds(z * LANES + b * BS, BS), pl.ds(c * LANES, LANES))
                    high[at], low[at] = split(value)
        return high, low

    for k in steps:
        for copy in copies[k]:
            copy.wait()
        high, low = unpack(k)
        left_high, left_low = split(lefts[k - first])
        total = jnp.dot(left_low, high[...], preferred_element_type=F32)
        total += jnp.dot(left_high, low[...], preferred_element_type=F32)
        total += jnp.dot(left_high, high[...], preferred_element_type=F32)
        if k == first and first:
            sum_copy.wait()
        if k:
            total += out[...]
        out[...] = total


def product(side, first, last, parts, where, packed, *before):
    smem = pl.BlockSpec(memory_space=pltpu.SMEM)
    hbm = pl.BlockSpec(memory_space=pltpu.HBM)
    vmem = pl.BlockSpec(memory_space=pltpu.VMEM)
    need = PACKED if side else META + 4 * LANES
    steps = last - first
    half = pltpu.VMEM((256, 512), BF)
    return pl.pallas_call(
        functools.partial(product_kernel, side, first, last),
        out_shape=jax.ShapeDtypeStruct((512, 512), F32),
        in_specs=[smem] + [hbm] * (1 + len(parts)) + [hbm] * len(before),
        out_specs=vmem,
        scratch_shapes=[
            pltpu.VMEM((steps, 2, need, LANES), F32),
            pltpu.VMEM((steps, 512, 256), F32),
            half,
            half,
            half,
            half,
            pltpu.SMEM((16, 1, LANES), F32),
            pltpu.SemaphoreType.DMA((steps,)),
            pltpu.SemaphoreType.DMA((steps,)),
            pltpu.SemaphoreType.DMA,
        ],
        cost_estimate=pl.CostEstimate(flops=6 * 512 * 512 * 256 * steps, bytes_accessed=steps << 20, transcendentals=0),
        compiler_params=pltpu.CompilerParams(vmem_limit_bytes=56 << 20),
    )(where, packed, *parts, *before)


def finish_kernel(side, where, flags, terms, square, *refs):
    out = refs[-1]
    for b in range(2):
        for c in range(4):
            at = (pl.ds(b * BS, BS), pl.ds(c * LANES, LANES))
            total = (terms[(0,) + at] + terms[(1,) + at]) + (terms[(2,) + at] + terms[(3,) + at])
            line, column = where[0] * 2 + b, 8 * side + 2 * c
            mask = pair_mask(flags[line, column], flags[line, column + 1])
            out[at] = mask * (3.0 * square[at] - 2.0 * total)


def finish(side, terms, square, flags, where, *before):
    smem = pl.BlockSpec(memory_space=pltpu.SMEM)
    half = pl.BlockSpec((128, 512), lambda i: (0, side))
    return pl.pallas_call(
        functools.partial(finish_kernel, side),
        out_shape=jax.ShapeDtypeStruct(square.shape, F32),
        grid=(1,),
        in_specs=[smem, smem, pl.BlockSpec((4, 128, 512), lambda i: (0, 0, 0)), half]
        + [pl.BlockSpec(memory_space=pltpu.HBM)] * len(before),
        out_specs=half,
        input_output_aliases={4: 0} if before else {},
        cost_estimate=pl.CostEstimate(flops=1 << 20, bytes_accessed=2 << 20, transcendentals=0),
    )(where, flags, terms, square, *before)


def shift(n, by):
    return [(i, (i + by) % n) for i in range(n)]


def gather_left(own):
    def send(x, by):
        return lax.ppermute(x, "col", shift(8, by))

    up1, down1 = send(own, 1), send(own, -1)
    far = send(own, 4)
    up2, down2 = send(up1, 1), send(down1, -1)
    up2, down2, far = lax.optimization_barrier((up2, down2, far))
    up3, down3 = send(up2, 1), send(down2, -1)
    return [own, up1, down1, up2, down2, far, up3, down3]


def local(left_slab, right_window, left_pattern, right_pattern, square_blocks, result_pattern):
    left, packed = prepare(left_slab[0], left_pattern[0].T, right_window[0], right_pattern[0])
    packed = lax.all_gather(packed, "row", axis=0, tiled=False)
    parts = gather_left(left)
    me = lax.axis_index("col")
    where = lax.rem(me + jnp.array([8, 7, 9, 6, 10, 12, 5, 11], jnp.int32), 8)
    layer = lax.axis_index("layer").reshape((1,))
    out = ()
    for side in range(2):
        if side:
            cube = product(side, 0, 8, parts, where, packed)
        else:
            cube = product(side, 0, 7, parts[:7], where, packed)
            cube = product(side, 7, 8, parts[7:], where, packed, cube)
        terms = lax.all_to_all(cube.reshape(4, 128, 512), "layer", 0, 0)
        out = (finish(side, terms, square_blocks, result_pattern, layer, *out),)
    return out[0]


def solution(mesh):
    in_specs = (
        P("layer", "row", "col"),
        P("layer", "row", "col"),
        P("layer", "row", "col"),
        P("layer", "row", "col"),
        P(("row", "layer"), "col"),
        P("row", "col"),
    )
    out_specs = P(("row", "layer"), "col")
    return jax.shard_map(local, mesh=mesh, in_specs=in_specs, out_specs=out_specs, check_vma=False)
```

```python
import functools

import jax
import jax.numpy as jnp
from jax import lax
from jax.experimental import pallas as pl
from jax.experimental.pallas import tpu as pltpu
from jax.sharding import PartitionSpec as P

BS = 64
LANES = 128
MAIN = 24
EXTRA = 8
META = 16
PACKED = META + 6 * LANES
BF = jnp.bfloat16
F32 = jnp.float32


def lane_half():
    return lax.broadcasted_iota(jnp.int32, (BS, LANES), 1) // BS


def pair_mask(low, high):
    return jnp.where(lane_half() == 0, low.astype(F32), high.astype(F32))


def prepare_kernel(left_flags, left, flags, x, left_out, out, holes):
    for i in range(8):
        for c in range(2):
            mask = pair_mask(left_flags[2 * c, i], left_flags[2 * c + 1, i])
            at = (pl.ds(i * BS, BS), pl.ds(c * LANES, LANES))
            left_out[at] = left[at] * mask
    for c in range(6):
        out[pl.ds(META + c * LANES, LANES), :] = x[:, pl.ds(c * LANES, LANES)]
    count = jnp.int32(0)
    for s in range(MAIN):
        holes[count] = s
        count = count + jnp.where(flags[(s >> 1) & 1, 2 * (s >> 2) + (s & 1)] == 0, 1, 0)
    used = jnp.int32(0)
    half = lane_half()
    lane = lax.broadcasted_iota(jnp.int32, (1, LANES), 1)
    row = jnp.zeros((1, LANES), F32)
    for e in range(EXTRA):
        kept = flags[e >> 2, 12 + (e & 3)] != 0
        slot = holes[jnp.minimum(used, EXTRA)]
        row = jnp.where(lane == e, jnp.where(kept, slot, -1).astype(F32), row)
        used = used + jnp.where(kept, 1, 0)

        @pl.when(kept)
        def _():
            at = pl.ds(pl.multiple_of(META + (slot >> 1) * BS, 16), BS)
            block = x[pl.ds((e >> 2) * BS, BS), pl.ds((6 + ((e >> 1) & 1)) * LANES, LANES)]
            side = slot & 1
            block = jnp.where(side == (e & 1), block, pltpu.roll(block, BS, 1))
            out[at, :] = jnp.where(half == side, block, out[at, :])

    out[pl.ds(0, 1), :] = row
    for c in range(6):
        for b in range(2):
            mask = jnp.where(lane < BS, flags[b, 2 * c].astype(F32), flags[b, 2 * c + 1].astype(F32))
            out[pl.ds(1 + c * 2 + b, 1), :] = mask
    out[pl.ds(13, 3), :] = jnp.zeros((3, LANES), F32)


def prepare(left, left_flags, right, right_flags):
    smem = pl.BlockSpec(memory_space=pltpu.SMEM)
    vmem = pl.BlockSpec(memory_space=pltpu.VMEM)
    return pl.pallas_call(
        prepare_kernel,
        out_shape=(jax.ShapeDtypeStruct(left.shape, F32), jax.ShapeDtypeStruct((PACKED, LANES), F32)),
        in_specs=[smem, vmem, smem, vmem],
        out_specs=(vmem, vmem),
        scratch_shapes=[pltpu.SMEM((MAIN + 1,), jnp.int32)],
    )(left_flags, left, right_flags, right)


def split(x):
    high = x.astype(BF)
    return high, (x - high.astype(F32)).astype(BF)


def product_kernel(side, first, last, where, packed, *refs):
    steps = range(first, last)
    parts, refs = refs[: last - first], refs[last - first :]
    out, tiles, lefts, high0, high1, low0, low1, homes, tile_sems, left_sems, home_sem = refs
    need = tiles.shape[2]
    copies = {}
    if side:
        home_copy = pltpu.make_async_copy(packed.at[:, pl.ds(0, 1), :], homes, home_sem)
        home_copy.start()
    for k in steps:
        n = k - first
        tile = pltpu.make_async_copy(packed.at[pl.ds(where[k] * 2, 2), pl.ds(0, need), :], tiles.at[n], tile_sems.at[n])
        tile.start()
        part = pltpu.make_async_copy(parts[n], lefts.at[n], left_sems.at[n])
        part.start()
        copies[k] = [tile, part]
    half = lane_half()
    if side:
        home_copy.wait()

    def unpack(k):
        n = k - first
        high, low = (high0, low0) if n % 2 == 0 else (high1, low1)
        for z in range(2):
            for b in range(2):
                for c in range(4):
                    pair = 4 * side + c
                    if pair < 6:
                        mask = tiles[n, z, pl.ds(1 + pair * 2 + b, 1), :]
                        value = tiles[n, z, pl.ds(META + pair * LANES + b * BS, BS), :] * mask
                    else:
                        halves = []
                        for h in range(2):
                            slot = homes[where[k] * 2 + z, 0, b * 4 + 2 * (pair - 6) + h].astype(jnp.int32)
                            kept = slot >= 0
                            slot = jnp.maximum(slot, 0)
                            block = tiles[n, z, pl.ds(pl.multiple_of(META + (slot >> 1) * BS, 16), BS), :]
                            block = jnp.where((slot & 1) == h, block, pltpu.roll(block, BS, 1))
                            halves.append(jnp.where(kept, block, 0.0))
                        value = jnp.where(half == 0, halves[0], halves[1])
                    at = (pl.ds(z * LANES + b * BS, BS), pl.ds(c * LANES, LANES))
                    high[at], low[at] = split(value)
        return high, low

    for k in steps:
        for copy in copies[k]:
            copy.wait()
        high, low = unpack(k)
        left_high, left_low = split(lefts[k - first])
        total = jnp.dot(left_low, high[...], preferred_element_type=F32)
        total += jnp.dot(left_high, low[...], preferred_element_type=F32)
        total += jnp.dot(left_high, high[...], preferred_element_type=F32)
        if k:
            total += out[...]
        out[...] = total


def product(side, first, last, parts, where, packed):
    smem = pl.BlockSpec(memory_space=pltpu.SMEM)
    hbm = pl.BlockSpec(memory_space=pltpu.HBM)
    vmem = pl.BlockSpec(memory_space=pltpu.VMEM)
    need = PACKED if side else META + 4 * LANES
    steps = last - first
    half = pltpu.VMEM((256, 512), BF)
    return pl.pallas_call(
        functools.partial(product_kernel, side, first, last),
        out_shape=jax.ShapeDtypeStruct((512, 512), F32),
        in_specs=[smem] + [hbm] * (1 + len(parts)),
        out_specs=vmem,
        scratch_shapes=[
            pltpu.VMEM((steps, 2, need, LANES), F32),
            pltpu.VMEM((steps, 512, 256), F32),
            half,
            half,
            half,
            half,
            pltpu.SMEM((16, 1, LANES), F32),
            pltpu.SemaphoreType.DMA((steps,)),
            pltpu.SemaphoreType.DMA((steps,)),
            pltpu.SemaphoreType.DMA,
        ],
        cost_estimate=pl.CostEstimate(flops=6 * 512 * 512 * 256 * steps, bytes_accessed=steps << 20, transcendentals=0),
        compiler_params=pltpu.CompilerParams(vmem_limit_bytes=56 << 20),
    )(where, packed, *parts)


def last_kernel(where, tiles, left, before, out, rights_high, rights_low):
    @pl.when(pl.program_id(0) == 0)
    def _():
        for z in range(2):
            for b in range(2):
                for c in range(4):
                    mask = tiles[z, pl.ds(1 + c * 2 + b, 1), :]
                    value = tiles[z, pl.ds(META + c * LANES + b * BS, BS), :] * mask
                    at = (pl.ds(z * LANES + b * BS, BS), pl.ds(c * LANES, LANES))
                    rights_high[at], rights_low[at] = split(value)

    left_high, left_low = split(left[...])
    total = jnp.dot(left_low, rights_high[...], preferred_element_type=F32)
    total += jnp.dot(left_high, rights_low[...], preferred_element_type=F32)
    total += jnp.dot(left_high, rights_high[...], preferred_element_type=F32)
    out[...] = before[...] + total


def add_last(part, where, packed, before):
    rows = pl.BlockSpec((256, 512), lambda i, where: (i, 0))
    return pl.pallas_call(
        last_kernel,
        out_shape=jax.ShapeDtypeStruct((512, 512), F32),
        grid_spec=pltpu.PrefetchScalarGridSpec(
            num_scalar_prefetch=1,
            grid=(2,),
            in_specs=[
                pl.BlockSpec((2, META + 4 * LANES, LANES), lambda i, where: (where[7], 0, 0)),
                pl.BlockSpec((256, 256), lambda i, where: (i, 0)),
                rows,
            ],
            out_specs=rows,
            scratch_shapes=[pltpu.VMEM((256, 512), BF)] * 2,
        ),
        cost_estimate=pl.CostEstimate(flops=6 * 512 * 512 * 256, bytes_accessed=3 << 20, transcendentals=0),
        compiler_params=pltpu.CompilerParams(vmem_limit_bytes=56 << 20),
    )(where, packed, part, before)


def finish_kernel(layer, flags, terms0, terms1, square, out):
    for b in range(2):
        for c in range(8):
            terms = terms1 if c >= 4 else terms0
            at = (pl.ds(b * BS, BS), pl.ds(c * LANES, LANES))
            near = (pl.ds(b * BS, BS), pl.ds(c % 4 * LANES, LANES))
            total = (terms[(0,) + near] + terms[(1,) + near]) + (terms[(2,) + near] + terms[(3,) + near])
            line = layer[0] * 2 + b
            mask = pair_mask(flags[line, 2 * c], flags[line, 2 * c + 1])
            out[at] = mask * (3.0 * square[at] - 2.0 * total)


def finish(terms, square, flags, layer):
    smem = pl.BlockSpec(memory_space=pltpu.SMEM)
    vmem = pl.BlockSpec(memory_space=pltpu.VMEM)
    return pl.pallas_call(
        finish_kernel,
        out_shape=jax.ShapeDtypeStruct(square.shape, F32),
        in_specs=[smem, smem, vmem, vmem, vmem],
        out_specs=vmem,
        cost_estimate=pl.CostEstimate(flops=1 << 20, bytes_accessed=3 << 20, transcendentals=0),
    )(layer, flags, *terms, square)


def shift(n, by):
    return [(i, (i + by) % n) for i in range(n)]


def gather_left(own):
    def send(x, by):
        return lax.ppermute(x, "col", shift(8, by))

    up1, down1 = send(own, 1), send(own, -1)
    up2, down2 = send(up1, 1), send(down1, -1)
    up3, down3 = send(up2, 1), send(down2, -1)
    return [own, up1, down1, up2, down2, up3, down3, send(up3, 1)]


def local(left_slab, right_window, left_pattern, right_pattern, square_blocks, result_pattern):
    left, packed = prepare(left_slab[0], left_pattern[0].T, right_window[0], right_pattern[0])
    packed = lax.all_gather(packed, "row", axis=0, tiled=False)
    parts = gather_left(left)
    me = lax.axis_index("col")
    where = lax.rem(me + jnp.array([8, 7, 9, 6, 10, 5, 11, 12], jnp.int32), 8)
    layer = lax.axis_index("layer").reshape((1,))
    cube = product(0, 0, 7, parts[:7], where, packed)
    cube = add_last(parts[7], where, packed, cube)
    terms = [lax.all_to_all(cube.reshape(4, 128, 512), "layer", 0, 0)]
    cube = product(1, 0, 8, parts, where, packed)
    terms.append(lax.all_to_all(cube.reshape(4, 128, 512), "layer", 0, 0))
    return finish(terms, square_blocks, result_pattern, layer)


def solution(mesh):
    in_specs = (
        P("layer", "row", "col"),
        P("layer", "row", "col"),
        P("layer", "row", "col"),
        P("layer", "row", "col"),
        P(("row", "layer"), "col"),
        P("row", "col"),
    )
    out_specs = P(("row", "layer"), "col")
    return jax.shard_map(local, mesh=mesh, in_specs=in_specs, out_specs=out_specs, check_vma=False)
```

```python
import functools

import jax
import jax.numpy as jnp
from jax import lax
from jax.experimental import pallas as pl
from jax.experimental.pallas import tpu as pltpu
from jax.sharding import PartitionSpec as P

BS = 64
LANES = 128
MAIN = 24
EXTRA = 8
META = 16
PACKED = META + 6 * LANES
ARRIVALS = (0, 7, 1, 6, 2, 5, 3, 4)
BF = jnp.bfloat16
F32 = jnp.float32


def lane_half():
    return lax.broadcasted_iota(jnp.int32, (BS, LANES), 1) // BS


def pair_mask(low, high):
    return jnp.where(lane_half() == 0, low.astype(F32), high.astype(F32))


def prepare_kernel(left_flags, left, flags, x, left_out, out, holes):
    for i in range(8):
        for c in range(2):
            mask = pair_mask(left_flags[2 * c, i], left_flags[2 * c + 1, i])
            at = (pl.ds(i * BS, BS), pl.ds(c * LANES, LANES))
            left_out[at] = left[at] * mask
    for c in range(6):
        out[pl.ds(META + c * LANES, LANES), :] = x[:, pl.ds(c * LANES, LANES)]
    count = jnp.int32(0)
    for s in range(MAIN):
        holes[count] = s
        count = count + jnp.where(flags[(s >> 1) & 1, 2 * (s >> 2) + (s & 1)] == 0, 1, 0)
    used = jnp.int32(0)
    half = lane_half()
    lane = lax.broadcasted_iota(jnp.int32, (1, LANES), 1)
    row = jnp.zeros((1, LANES), F32)
    for e in range(EXTRA):
        kept = flags[e >> 2, 12 + (e & 3)] != 0
        slot = holes[jnp.minimum(used, EXTRA)]
        row = jnp.where(lane == e, jnp.where(kept, slot, -1).astype(F32), row)
        used = used + jnp.where(kept, 1, 0)

        @pl.when(kept)
        def _():
            at = pl.ds(pl.multiple_of(META + (slot >> 1) * BS, 16), BS)
            block = x[pl.ds((e >> 2) * BS, BS), pl.ds((6 + ((e >> 1) & 1)) * LANES, LANES)]
            side = slot & 1
            block = jnp.where(side == (e & 1), block, pltpu.roll(block, BS, 1))
            out[at, :] = jnp.where(half == side, block, out[at, :])

    out[pl.ds(0, 1), :] = row
    for c in range(6):
        for b in range(2):
            mask = jnp.where(lane < BS, flags[b, 2 * c].astype(F32), flags[b, 2 * c + 1].astype(F32))
            out[pl.ds(1 + c * 2 + b, 1), :] = mask
    out[pl.ds(13, 3), :] = jnp.zeros((3, LANES), F32)


def prepare(left, left_flags, right, right_flags):
    smem = pl.BlockSpec(memory_space=pltpu.SMEM)
    vmem = pl.BlockSpec(memory_space=pltpu.VMEM)
    return pl.pallas_call(
        prepare_kernel,
        out_shape=(jax.ShapeDtypeStruct(left.shape, F32), jax.ShapeDtypeStruct((PACKED, LANES), F32)),
        in_specs=[smem, vmem, smem, vmem],
        out_specs=(vmem, vmem),
        scratch_shapes=[pltpu.SMEM((MAIN + 1,), jnp.int32)],
    )(left_flags, left, right_flags, right)


def split(x):
    high = x.astype(BF)
    return high, (x - high.astype(F32)).astype(BF)


def product_kernel(side, first, last, me, packed, *refs):
    steps = range(first, last)
    where = [(me[0] + by) & 7 for by in ARRIVALS]
    parts, refs = refs[: last - first], refs[last - first :]
    out, tiles, lefts, high0, high1, low0, low1, homes, tile_sems, left_sems, home_sem = refs
    need = tiles.shape[2]
    copies = {}
    if side:
        home_copy = pltpu.make_async_copy(packed.at[:, pl.ds(0, 1), :], homes, home_sem)
        home_copy.start()
    for k in steps:
        n = k - first
        tile = pltpu.make_async_copy(packed.at[pl.ds(where[k] * 2, 2), pl.ds(0, need), :], tiles.at[n], tile_sems.at[n])
        tile.start()
        part = pltpu.make_async_copy(parts[n], lefts.at[n], left_sems.at[n])
        part.start()
        copies[k] = [tile, part]
    half = lane_half()
    if side:
        home_copy.wait()

    def unpack(k):
        n = k - first
        high, low = (high0, low0) if n % 2 == 0 else (high1, low1)
        for z in range(2):
            for b in range(2):
                for c in range(4):
                    pair = 4 * side + c
                    if pair < 6:
                        mask = tiles[n, z, pl.ds(1 + pair * 2 + b, 1), :]
                        value = tiles[n, z, pl.ds(META + pair * LANES + b * BS, BS), :] * mask
                    else:
                        halves = []
                        for h in range(2):
                            slot = homes[where[k] * 2 + z, 0, b * 4 + 2 * (pair - 6) + h].astype(jnp.int32)
                            kept = slot >= 0
                            slot = jnp.maximum(slot, 0)
                            block = tiles[n, z, pl.ds(pl.multiple_of(META + (slot >> 1) * BS, 16), BS), :]
                            block = jnp.where((slot & 1) == h, block, pltpu.roll(block, BS, 1))
                            halves.append(jnp.where(kept, block, 0.0))
                        value = jnp.where(half == 0, halves[0], halves[1])
                    at = (pl.ds(z * LANES + b * BS, BS), pl.ds(c * LANES, LANES))
                    high[at], low[at] = split(value)
        return high, low

    for k in steps:
        for copy in copies[k]:
            copy.wait()
        high, low = unpack(k)
        left_high, left_low = split(lefts[k - first])
        total = jnp.dot(left_low, high[...], preferred_element_type=F32)
        total += jnp.dot(left_high, low[...], preferred_element_type=F32)
        total += jnp.dot(left_high, high[...], preferred_element_type=F32)
        if k:
            total += out[...]
        out[...] = total


def product(side, first, last, parts, me, packed):
    smem = pl.BlockSpec(memory_space=pltpu.SMEM)
    hbm = pl.BlockSpec(memory_space=pltpu.HBM)
    vmem = pl.BlockSpec(memory_space=pltpu.VMEM)
    need = PACKED if side else META + 4 * LANES
    steps = last - first
    half = pltpu.VMEM((256, 512), BF)
    return pl.pallas_call(
        functools.partial(product_kernel, side, first, last),
        out_shape=jax.ShapeDtypeStruct((512, 512), F32),
        in_specs=[smem] + [hbm] * (1 + len(parts)),
        out_specs=vmem,
        scratch_shapes=[
            pltpu.VMEM((steps, 2, need, LANES), F32),
            pltpu.VMEM((steps, 512, 256), F32),
            half,
            half,
            half,
            half,
            pltpu.SMEM((16, 1, LANES), F32),
            pltpu.SemaphoreType.DMA((steps,)),
            pltpu.SemaphoreType.DMA((steps,)),
            pltpu.SemaphoreType.DMA,
        ],
        cost_estimate=pl.CostEstimate(flops=6 * 512 * 512 * 256 * steps, bytes_accessed=steps << 20, transcendentals=0),
        compiler_params=pltpu.CompilerParams(vmem_limit_bytes=56 << 20),
    )(me, packed, *parts)


def last_kernel(me, tiles, left, before, out, rights_high, rights_low):
    @pl.when(pl.program_id(0) == 0)
    def _():
        for z in range(2):
            for b in range(2):
                for c in range(4):
                    mask = tiles[z, pl.ds(1 + c * 2 + b, 1), :]
                    value = tiles[z, pl.ds(META + c * LANES + b * BS, BS), :] * mask
                    at = (pl.ds(z * LANES + b * BS, BS), pl.ds(c * LANES, LANES))
                    rights_high[at], rights_low[at] = split(value)

    left_high, left_low = split(left[...])
    total = jnp.dot(left_low, rights_high[...], preferred_element_type=F32)
    total += jnp.dot(left_high, rights_low[...], preferred_element_type=F32)
    total += jnp.dot(left_high, rights_high[...], preferred_element_type=F32)
    out[...] = before[...] + total


def add_last(part, me, packed, before):
    rows = pl.BlockSpec((256, 512), lambda i, me: (i, 0))
    return pl.pallas_call(
        last_kernel,
        out_shape=jax.ShapeDtypeStruct((512, 512), F32),
        grid_spec=pltpu.PrefetchScalarGridSpec(
            num_scalar_prefetch=1,
            grid=(2,),
            in_specs=[
                pl.BlockSpec((2, META + 4 * LANES, LANES), lambda i, me: ((me[0] + ARRIVALS[7]) & 7, 0, 0)),
                pl.BlockSpec((256, 256), lambda i, me: (i, 0)),
                rows,
            ],
            out_specs=rows,
            scratch_shapes=[pltpu.VMEM((256, 512), BF)] * 2,
        ),
        cost_estimate=pl.CostEstimate(flops=6 * 512 * 512 * 256, bytes_accessed=3 << 20, transcendentals=0),
        compiler_params=pltpu.CompilerParams(vmem_limit_bytes=56 << 20),
    )(me, packed, part, before)


def finish_kernel(side, where, flags, terms, square, *refs):
    out = refs[-1]
    for b in range(2):
        for c in range(4):
            at = (pl.ds(b * BS, BS), pl.ds(c * LANES, LANES))
            total = (terms[(0,) + at] + terms[(1,) + at]) + (terms[(2,) + at] + terms[(3,) + at])
            line, column = where[0] * 2 + b, 8 * side + 2 * c
            mask = pair_mask(flags[line, column], flags[line, column + 1])
            out[at] = mask * (3.0 * square[at] - 2.0 * total)


def finish(side, terms, square, flags, where, *before):
    smem = pl.BlockSpec(memory_space=pltpu.SMEM)
    half = pl.BlockSpec((128, 512), lambda i: (0, side))
    return pl.pallas_call(
        functools.partial(finish_kernel, side),
        out_shape=jax.ShapeDtypeStruct(square.shape, F32),
        grid=(1,),
        in_specs=[smem, smem, pl.BlockSpec((4, 128, 512), lambda i: (0, 0, 0)), half]
        + [pl.BlockSpec(memory_space=pltpu.HBM)] * len(before),
        out_specs=half,
        input_output_aliases={4: 0} if before else {},
        cost_estimate=pl.CostEstimate(flops=1 << 20, bytes_accessed=2 << 20, transcendentals=0),
    )(where, flags, terms, square, *before)


def shift(n, by):
    return [(i, (i + by) % n) for i in range(n)]


def gather_left(own):
    def send(x, by):
        return lax.ppermute(x, "col", shift(8, by))

    up1, down1 = send(own, 1), send(own, -1)
    up2, down2 = send(up1, 1), send(down1, -1)
    up3, down3 = send(up2, 1), send(down2, -1)
    return [own, up1, down1, up2, down2, up3, down3, send(up3, 1)]


def local(left_slab, right_window, left_pattern, right_pattern, square_blocks, result_pattern):
    left, packed = prepare(left_slab[0], left_pattern[0].T, right_window[0], right_pattern[0])
    packed = lax.all_gather(packed, "row", axis=0, tiled=False)
    parts = gather_left(left)
    me = lax.axis_index("col").reshape((1,))
    layer = lax.axis_index("layer").reshape((1,))
    cube = product(0, 0, 7, parts[:7], me, packed)
    cube = add_last(parts[7], me, packed, cube)
    me, cube = lax.optimization_barrier((me, cube))
    terms = lax.all_to_all(cube.reshape(4, 128, 512), "layer", 0, 0)
    out = finish(0, terms, square_blocks, result_pattern, layer)
    cube = product(1, 0, 8, parts, me, packed)
    terms = lax.all_to_all(cube.reshape(4, 128, 512), "layer", 0, 0)
    return finish(1, terms, square_blocks, result_pattern, layer, out)


def solution(mesh):
    in_specs = (
        P("layer", "row", "col"),
        P("layer", "row", "col"),
        P("layer", "row", "col"),
        P("layer", "row", "col"),
        P(("row", "layer"), "col"),
        P("row", "col"),
    )
    out_specs = P(("row", "layer"), "col")
    return jax.shard_map(local, mesh=mesh, in_specs=in_specs, out_specs=out_specs, check_vma=False)
```

```python
import functools

import jax
import jax.numpy as jnp
from jax import lax
from jax.experimental import pallas as pl
from jax.experimental.pallas import tpu as pltpu
from jax.sharding import PartitionSpec as P

BS = 64
LANES = 128
MAIN = 24
EXTRA = 8
META = 16
PACKED = META + 6 * LANES
ARRIVALS = (0, 7, 1, 6, 2, 5, 3, 4)
BF = jnp.bfloat16
F32 = jnp.float32


def lane_half():
    return lax.broadcasted_iota(jnp.int32, (BS, LANES), 1) // BS


def pair_mask(low, high):
    return jnp.where(lane_half() == 0, low.astype(F32), high.astype(F32))


def prepare_kernel(left_flags, left, flags, x, left_out, out, holes):
    for i in range(8):
        for c in range(2):
            mask = pair_mask(left_flags[2 * c, i], left_flags[2 * c + 1, i])
            at = (pl.ds(i * BS, BS), pl.ds(c * LANES, LANES))
            left_out[at] = left[at] * mask
    for c in range(6):
        out[pl.ds(META + c * LANES, LANES), :] = x[:, pl.ds(c * LANES, LANES)]
    count = jnp.int32(0)
    for s in range(MAIN):
        holes[count] = s
        count = count + jnp.where(flags[(s >> 1) & 1, 2 * (s >> 2) + (s & 1)] == 0, 1, 0)
    used = jnp.int32(0)
    half = lane_half()
    lane = lax.broadcasted_iota(jnp.int32, (1, LANES), 1)
    row = jnp.zeros((1, LANES), F32)
    for e in range(EXTRA):
        kept = flags[e >> 2, 12 + (e & 3)] != 0
        slot = holes[jnp.minimum(used, EXTRA)]
        row = jnp.where(lane == e, jnp.where(kept, slot, -1).astype(F32), row)
        used = used + jnp.where(kept, 1, 0)

        @pl.when(kept)
        def _():
            at = pl.ds(pl.multiple_of(META + (slot >> 1) * BS, 16), BS)
            block = x[pl.ds((e >> 2) * BS, BS), pl.ds((6 + ((e >> 1) & 1)) * LANES, LANES)]
            side = slot & 1
            block = jnp.where(side == (e & 1), block, pltpu.roll(block, BS, 1))
            out[at, :] = jnp.where(half == side, block, out[at, :])

    out[pl.ds(0, 1), :] = row
    for c in range(6):
        for b in range(2):
            mask = jnp.where(lane < BS, flags[b, 2 * c].astype(F32), flags[b, 2 * c + 1].astype(F32))
            out[pl.ds(1 + c * 2 + b, 1), :] = mask
    out[pl.ds(13, 3), :] = jnp.zeros((3, LANES), F32)


def prepare(left, left_flags, right, right_flags):
    smem = pl.BlockSpec(memory_space=pltpu.SMEM)
    vmem = pl.BlockSpec(memory_space=pltpu.VMEM)
    return pl.pallas_call(
        prepare_kernel,
        out_shape=(jax.ShapeDtypeStruct(left.shape, F32), jax.ShapeDtypeStruct((PACKED, LANES), F32)),
        in_specs=[smem, vmem, smem, vmem],
        out_specs=(vmem, vmem),
        scratch_shapes=[pltpu.SMEM((MAIN + 1,), jnp.int32)],
    )(left_flags, left, right_flags, right)


def split(x):
    high = x.astype(BF)
    return high, (x - high.astype(F32)).astype(BF)


def product_kernel(side, first, last, me, packed, *refs):
    steps = range(first, last)
    where = [(me[0] + by) & 7 for by in ARRIVALS]
    parts, refs = refs[: last - first], refs[last - first :]
    out, tiles, lefts, high0, high1, low0, low1, homes, tile_sems, left_sems, home_sem = refs
    need = tiles.shape[2]
    copies = {}
    if side:
        home_copy = pltpu.make_async_copy(packed.at[:, pl.ds(0, 1), :], homes, home_sem)
        home_copy.start()
    for k in steps:
        n = k - first
        tile = pltpu.make_async_copy(packed.at[pl.ds(where[k] * 2, 2), pl.ds(0, need), :], tiles.at[n], tile_sems.at[n])
        tile.start()
        part = pltpu.make_async_copy(parts[n], lefts.at[n], left_sems.at[n])
        part.start()
        copies[k] = [tile, part]
    half = lane_half()
    if side:
        home_copy.wait()

    def unpack(k):
        n = k - first
        high, low = (high0, low0) if n % 2 == 0 else (high1, low1)
        for z in range(2):
            for b in range(2):
                for c in range(4):
                    pair = 4 * side + c
                    if pair < 6:
                        mask = tiles[n, z, pl.ds(1 + pair * 2 + b, 1), :]
                        value = tiles[n, z, pl.ds(META + pair * LANES + b * BS, BS), :] * mask
                    else:
                        halves = []
                        for h in range(2):
                            slot = homes[where[k] * 2 + z, 0, b * 4 + 2 * (pair - 6) + h].astype(jnp.int32)
                            kept = slot >= 0
                            slot = jnp.maximum(slot, 0)
                            block = tiles[n, z, pl.ds(pl.multiple_of(META + (slot >> 1) * BS, 16), BS), :]
                            block = jnp.where((slot & 1) == h, block, pltpu.roll(block, BS, 1))
                            halves.append(jnp.where(kept, block, 0.0))
                        value = jnp.where(half == 0, halves[0], halves[1])
                    at = (pl.ds(z * LANES + b * BS, BS), pl.ds(c * LANES, LANES))
                    high[at], low[at] = split(value)
        return high, low

    for k in steps:
        for copy in copies[k]:
            copy.wait()
        high, low = unpack(k)
        left_high, left_low = split(lefts[k - first])
        total = jnp.dot(left_low, high[...], preferred_element_type=F32)
        total += jnp.dot(left_high, low[...], preferred_element_type=F32)
        total += jnp.dot(left_high, high[...], preferred_element_type=F32)
        if k:
            total += out[...]
        out[...] = total


def product(side, first, last, parts, me, packed):
    smem = pl.BlockSpec(memory_space=pltpu.SMEM)
    hbm = pl.BlockSpec(memory_space=pltpu.HBM)
    vmem = pl.BlockSpec(memory_space=pltpu.VMEM)
    need = PACKED if side else META + 4 * LANES
    steps = last - first
    half = pltpu.VMEM((256, 512), BF)
    return pl.pallas_call(
        functools.partial(product_kernel, side, first, last),
        out_shape=jax.ShapeDtypeStruct((512, 512), F32),
        in_specs=[smem] + [hbm] * (1 + len(parts)),
        out_specs=vmem,
        scratch_shapes=[
            pltpu.VMEM((steps, 2, need, LANES), F32),
            pltpu.VMEM((steps, 512, 256), F32),
            half,
            half,
            half,
            half,
            pltpu.SMEM((16, 1, LANES), F32),
            pltpu.SemaphoreType.DMA((steps,)),
            pltpu.SemaphoreType.DMA((steps,)),
            pltpu.SemaphoreType.DMA,
        ],
        cost_estimate=pl.CostEstimate(flops=6 * 512 * 512 * 256 * steps, bytes_accessed=steps << 20, transcendentals=0),
        compiler_params=pltpu.CompilerParams(vmem_limit_bytes=56 << 20),
    )(me, packed, *parts)


def last_kernel(me, tiles, left, before, out, rights_high, rights_low):
    @pl.when(pl.program_id(0) == 0)
    def _():
        for z in range(2):
            for b in range(2):
                for c in range(4):
                    mask = tiles[z, pl.ds(1 + c * 2 + b, 1), :]
                    value = tiles[z, pl.ds(META + c * LANES + b * BS, BS), :] * mask
                    at = (pl.ds(z * LANES + b * BS, BS), pl.ds(c * LANES, LANES))
                    rights_high[at], rights_low[at] = split(value)

    left_high, left_low = split(left[...])
    total = jnp.dot(left_low, rights_high[...], preferred_element_type=F32)
    total += jnp.dot(left_high, rights_low[...], preferred_element_type=F32)
    total += jnp.dot(left_high, rights_high[...], preferred_element_type=F32)
    out[...] = before[...] + total


def add_last(part, me, packed, before):
    rows = pl.BlockSpec((256, 512), lambda i, me: (i, 0))
    return pl.pallas_call(
        last_kernel,
        out_shape=jax.ShapeDtypeStruct((512, 512), F32),
        grid_spec=pltpu.PrefetchScalarGridSpec(
            num_scalar_prefetch=1,
            grid=(2,),
            in_specs=[
                pl.BlockSpec((2, META + 4 * LANES, LANES), lambda i, me: ((me[0] + ARRIVALS[7]) & 7, 0, 0)),
                pl.BlockSpec((256, 256), lambda i, me: (i, 0)),
                rows,
            ],
            out_specs=rows,
            scratch_shapes=[pltpu.VMEM((256, 512), BF)] * 2,
        ),
        cost_estimate=pl.CostEstimate(flops=6 * 512 * 512 * 256, bytes_accessed=3 << 20, transcendentals=0),
        compiler_params=pltpu.CompilerParams(vmem_limit_bytes=56 << 20),
    )(me, packed, part, before)


def finish_kernel(side, where, flags, terms, square, *refs):
    out = refs[-1]
    for b in range(2):
        for c in range(4):
            at = (pl.ds(b * BS, BS), pl.ds(c * LANES, LANES))
            total = (terms[(0,) + at] + terms[(1,) + at]) + (terms[(2,) + at] + terms[(3,) + at])
            line, column = where[0] * 2 + b, 8 * side + 2 * c
            mask = pair_mask(flags[line, column], flags[line, column + 1])
            out[at] = mask * (3.0 * square[at] - 2.0 * total)


def finish(side, terms, square, flags, where, *before):
    smem = pl.BlockSpec(memory_space=pltpu.SMEM)
    half = pl.BlockSpec((128, 512), lambda i: (0, side))
    return pl.pallas_call(
        functools.partial(finish_kernel, side),
        out_shape=jax.ShapeDtypeStruct(square.shape, F32),
        grid=(1,),
        in_specs=[smem, smem, pl.BlockSpec(memory_space=pltpu.VMEM), half]
        + [pl.BlockSpec(memory_space=pltpu.HBM)] * len(before),
        out_specs=half,
        input_output_aliases={4: 0} if before else {},
        cost_estimate=pl.CostEstimate(flops=1 << 20, bytes_accessed=2 << 20, transcendentals=0),
    )(where, flags, terms, square, *before)


def shift(n, by):
    return [(i, (i + by) % n) for i in range(n)]


def gather_left(own):
    def send(x, by):
        return lax.ppermute(x, "col", shift(8, by))

    up1, down1 = send(own, 1), send(own, -1)
    up2, down2 = send(up1, 1), send(down1, -1)
    up3, down3 = send(up2, 1), send(down2, -1)
    return [own, up1, down1, up2, down2, up3, down3, send(up3, 1)]


def local(left_slab, right_window, left_pattern, right_pattern, square_blocks, result_pattern):
    left, packed = prepare(left_slab[0], left_pattern[0].T, right_window[0], right_pattern[0])
    packed = lax.all_gather(packed, "row", axis=0, tiled=False)
    parts = gather_left(left)
    me = lax.axis_index("col").reshape((1,))
    layer = lax.axis_index("layer").reshape((1,))
    cube = product(0, 0, 7, parts[:7], me, packed)
    cube = add_last(parts[7], me, packed, cube)
    me, cube = lax.optimization_barrier((me, cube))
    terms = lax.all_to_all(cube.reshape(4, 128, 512), "layer", 0, 0)
    out = finish(0, terms, square_blocks, result_pattern, layer)
    cube = product(1, 0, 8, parts, me, packed)
    terms = lax.all_to_all(cube.reshape(4, 128, 512), "layer", 0, 0)
    return finish(1, terms, square_blocks, result_pattern, layer, out)


def solution(mesh):
    in_specs = (
        P("layer", "row", "col"),
        P("layer", "row", "col"),
        P("layer", "row", "col"),
        P("layer", "row", "col"),
        P(("row", "layer"), "col"),
        P("row", "col"),
    )
    out_specs = P(("row", "layer"), "col")
    return jax.shard_map(local, mesh=mesh, in_specs=in_specs, out_specs=out_specs, check_vma=False)
```
